256 devices in a mesh: dom: 64 (over z, x_hi, y), orb: 4 (over x_lo, core).
Axes of the slice: x: 4 (x_hi: 2, x_lo: 2; x = x_hi * 2 + x_lo), y: 4, z: 8, core: 2. Of those that a mesh axis runs over, the one named last changes fastest.
Arguments:
- y_prev: bfloat16 [65536, 512], P('dom', 'orb'), may hold values from -6 to 6
- y_cur: bfloat16 [65536, 512], P('dom', 'orb'), may hold values from -6 to 6
- others: bfloat16 [65536, 3584], P('dom', 'orb'), may hold values from -6 to 6
- potential: bfloat16 [65536], P('dom'), may hold values from -1.5 to 1.5
- stiffness: bfloat16 [343, 343], replicated, may hold values from -1 to 2
- cell_scale: float32 [256], P('dom'), may hold values from 0.5 to 2
- connectivity: int32 [256, 343], P('dom'), may hold values from 0 to 1151, as said below
- boundary: int32 [128, 64], P('dom'), may hold values from -1 to 1023, as said below
- rotation: bfloat16 [4096, 4096], P('orb', 'dom'), may hold values from -0.09375 to 0.09375
- panel_ids: int32 [4], replicated, may hold values from 0 to 63
Outputs:
- y_next: bfloat16 [65536, 512], P('dom', 'orb')
- rotated: bfloat16 [65536, 256], P(('dom', 'orb'))
The draws below stay inside these ranges and needn't reach their ends.
Inputs may be any that keep to these rules, and one draw needn't show every extreme that they name: `boundary`: row 2 d lists the owned rows of partition d that partition d - 1 uses, row 2 d + 1 those that partition d + 1 uses. Live entries come first and are distinct, the two rows of a partition share no entry, and padding is -1. The first partition sends nothing down and the last nothing up; in every draw some partition fills each direction's 64 slots. `connectivity`: each cell names 343 distinct slots of its partition's extended node list: owned rows 0 to 1023, then 64 ghost slots whose j-th is entry j of the lower partition's upper list, then 64 ghost slots whose j-th is entry j of the upper partition's lower list. Only live ghost slots are named, and every owned row and live ghost slot is named by some cell of the partition. No slot is named by more than 2 cells of its partition, and in every draw some slot is named by exactly 2.
All inputs are finite; a program needn't handle non-finite values.
Results may differ from the reference program's by a relative error of at most 0.0062.
Values may be sent and summed in bfloat16 or wider, within the bound.
No kernel may reach another device: no remote copies, remote signals or barrier semaphores. Data moves between devices by JAX's collectives and lax.ppermute only.
A program may use at most 64 MiB of HBM per device.

```python
import math
import jax
import jax.numpy as jnp
from jax import lax

SUB = 4096
BLOCK = 512
PANEL = 64
PANELS = 4
STEPS = 4
NPC = 343
NODES_DEV = 1024
CELLS_DEV = 4
BND = 64
SLICES = 4
NODES = 65536
CELLS = 256
N_DOM = 64


def draw_stiffness(key, part):
    base = jnp.clip(jax.random.normal(key, (NPC, NPC), jnp.float32), -4.0, 4.0)
    coupled = (base + base.T) * (0.7 / math.sqrt(NPC))
    return (coupled + jnp.eye(NPC, dtype=jnp.float32)).astype(jnp.bfloat16)


def mesh_layout(key):
    keys = jax.random.split(jax.random.fold_in(key, 11), 6)
    device = jnp.arange(N_DOM, dtype=jnp.int32)
    up_count = jax.random.randint(keys[0], (N_DOM,), BND // 2, BND + 1)
    up_full = jax.random.randint(keys[1], (), 0, N_DOM - 1)
    up_count = jnp.where(device == up_full, BND, up_count)
    up_count = jnp.where(device == N_DOM - 1, 0, up_count)
    down_count = jax.random.randint(keys[2], (N_DOM,), BND // 2, BND + 1)
    down_full = jax.random.randint(keys[3], (), 1, N_DOM)
    down_count = jnp.where(device == down_full, BND, down_count)
    down_count = jnp.where(device == 0, 0, down_count)
    orders = jax.vmap(lambda single: jax.random.permutation(single, NODES_DEV))(jax.random.split(keys[4], N_DOM)).astype(jnp.int32)
    slot = jnp.arange(BND, dtype=jnp.int32)[None, :]
    down_list = jnp.where(slot < down_count[:, None], orders[:, :BND], -1)
    up_list = jnp.where(slot < up_count[:, None], orders[:, BND:2 * BND], -1)
    boundary = jnp.stack([down_list, up_list], axis=1).reshape(N_DOM * 2, BND).astype(jnp.int32)
    lower_live = jnp.roll(up_count, 1)
    upper_live = jnp.roll(down_count, -1)
    extent = NODES_DEV + 2 * BND
    position = jnp.arange(extent, dtype=jnp.int32)[None, :]
    in_lower = (position >= NODES_DEV) & (position < NODES_DEV + lower_live[:, None])
    in_upper = (position >= NODES_DEV + BND) & (position < NODES_DEV + BND + upper_live[:, None])
    live = (position < NODES_DEV) | in_lower | in_upper
    noise = jax.random.randint(keys[5], (N_DOM, extent), 0, 65536)
    scores = noise * extent + position + jnp.where(live, 0, 1 << 30)
    ranked = jnp.argsort(scores, axis=1, stable=True).astype(jnp.int32)
    live_count = NODES_DEV + lower_live + upper_live
    entry = jnp.arange(CELLS_DEV * NPC, dtype=jnp.int32)[None, :] % live_count[:, None]
    cells = jnp.take_along_axis(ranked, entry, axis=1)
    return (cells.reshape(N_DOM * CELLS_DEV, NPC).astype(jnp.int32), boundary)


def draw_connectivity(key, part):
    return mesh_layout(key)[0]


def draw_boundary(key, part):
    return mesh_layout(key)[1]


def with_ends(result, key, low, high):
    shape = result.shape
    place = [jax.random.randint(jax.random.fold_in(key, axis), (), 0, shape[axis]) for axis in range(len(shape))]
    result = result.at[tuple(place)].set(low)
    longest = shape.index(max(shape))
    place[longest] = (place[longest] + 1) % shape[longest]
    return result.at[tuple(place)].set(high)


def level_of(key, shape, cuts, least, top_value):
    def one(dim, blocks):
        steps = jax.random.uniform(jax.random.fold_in(jax.random.fold_in(key, 6), dim), (blocks,), jnp.float32, least / len(cuts), top_value / len(cuts))
        return jnp.repeat(jnp.exp(steps), shape[dim] // blocks).reshape((-1,) + (1,) * (len(shape) - dim - 1))

    level = one(*cuts[0])
    for cut in cuts[1:]:
        level = level * one(*cut)
    return level


def scatter_about(rng, dims, deviation, reach, cuts=(), kind=jnp.bfloat16):
    result = jax.random.normal(rng, dims, jnp.float32) * deviation
    if len(cuts) > 0:
        result = level_of(rng, dims, cuts, -0.22, 0.18) * result
    return jnp.clip(result, min=-reach, max=reach).astype(kind)


def setup_inputs(seed: int = 0) -> dict:
    splits = jax.random.split(jax.random.key(seed), 11)
    y_prev = scatter_about(splits[0], (NODES, BLOCK), 1.0, 6.0, ((0, 64), (1, 4)))
    y_cur = scatter_about(splits[1], (NODES, BLOCK), 1.0, 6.0, ((0, 64), (1, 4)))
    others = scatter_about(splits[2], (NODES, SUB - BLOCK), 1.0, 6.0, ((0, 64), (1, 4)))
    potential = jnp.clip(jax.random.uniform(splits[3], (NODES,), jnp.float32, -1.5, 1.5) * level_of(splits[3], (NODES,), ((0, 64),), -0.4, 0.0), -1.5, 1.5).astype(jnp.bfloat16)
    stiffness = draw_stiffness(jax.random.fold_in(splits[10], 71), 0)
    cell_scale = jnp.clip(jnp.exp(math.log(2.0) - 1.3862944 * jax.random.uniform(splits[5], (CELLS,), jnp.float32) ** level_of(splits[5], (CELLS,), ((0, 64),), -0.2, 0.2)), 0.5, 2.0)
    connectivity = draw_connectivity(jax.random.fold_in(splits[10], 71), 0)
    boundary = draw_boundary(jax.random.fold_in(splits[10], 71), 0)
    rotation = scatter_about(splits[8], (SUB, SUB), SUB ** -0.5, 0.09375, ((0, 4), (1, 64)))
    panel_ids = with_ends(jax.random.randint(splits[9], (PANELS,), 0, SUB // PANEL), jax.random.fold_in(splits[9], 1), 0, (SUB // PANEL) - 1).astype(jnp.int32)
    return dict(y_prev=y_prev, y_cur=y_cur, others=others, potential=potential, stiffness=stiffness, cell_scale=cell_scale, connectivity=connectivity, boundary=boundary, rotation=rotation, panel_ids=panel_ids)


CENTER = 0.5
SCALE = 0.5


def global_cells(connectivity, boundary):
    lists = boundary.reshape(N_DOM, 2, BND)
    from_lower = jnp.roll(lists[:, 1, :], 1, axis=0)
    from_upper = jnp.roll(lists[:, 0, :], -1, axis=0)
    slots = connectivity.reshape(N_DOM, CELLS_DEV * NPC)
    device = jnp.arange(N_DOM, dtype=jnp.int32)[:, None]
    low_slot = jnp.clip(slots - NODES_DEV, 0, BND - 1)
    high_slot = jnp.clip(slots - NODES_DEV - BND, 0, BND - 1)
    low_node = jnp.take_along_axis(from_lower, low_slot, axis=1)
    high_node = jnp.take_along_axis(from_upper, high_slot, axis=1)
    owned = device * NODES_DEV + slots
    lower = (device - 1) * NODES_DEV + low_node
    upper = (device + 1) * NODES_DEV + high_node
    nodes = jnp.where(slots < NODES_DEV, owned, jnp.where(slots < NODES_DEV + BND, lower, upper))
    return nodes.reshape(N_DOM, CELLS_DEV, NPC).astype(jnp.int32)


def apply_h(field, cell_nodes, stiffness, cell_scale, potential):
    columns = field.shape[1]
    scales = cell_scale.reshape(N_DOM, CELLS_DEV)

    def add_block(total, block):
        nodes, scale = block
        index_rows = nodes.T.reshape(-1)
        local = jnp.take(field, index_rows, axis=0).reshape(NPC, CELLS_DEV * columns)
        product = jnp.dot(stiffness, local, preferred_element_type=jnp.float32)
        product = product.reshape(NPC, CELLS_DEV, columns) * scale[None, :, None]
        return total.at[index_rows].add(product.reshape(-1, columns)), None

    total, _ = lax.scan(add_block, jnp.zeros(field.shape, jnp.float32), (cell_nodes, scales))
    return total + potential.astype(jnp.float32)[:, None] * field.astype(jnp.float32)


def next_block(applied, current, previous):
    return (SCALE * (applied - CENTER * current.astype(jnp.float32)) - previous.astype(jnp.float32)).astype(jnp.bfloat16)


def reference(y_prev, y_cur, others, potential, stiffness, cell_scale, connectivity, boundary, rotation, panel_ids):
    cell_nodes = global_cells(connectivity, boundary)
    previous, current = y_prev, y_cur
    for step in range(STEPS):
        applied = apply_h(current, cell_nodes, stiffness, cell_scale, potential)
        current, previous = next_block(applied, current, previous), current
    firsts = (panel_ids * PANEL).astype(jnp.int32)
    columns = [lax.dynamic_slice_in_dim(rotation, firsts[order], PANEL, 1) for order in range(PANELS)]
    panel_cols = jnp.concatenate(columns, axis=1)
    grouped = panel_cols.reshape(SLICES, SUB // SLICES, PANELS * PANEL)
    block_rows = grouped[:, : BLOCK // SLICES].reshape(BLOCK, PANELS * PANEL)
    other_rows = grouped[:, BLOCK // SLICES:].reshape(SUB - BLOCK, PANELS * PANEL)
    rotated = jnp.dot(current, block_rows, preferred_element_type=jnp.float32) + jnp.dot(others, other_rows, preferred_element_type=jnp.float32)
    return current, rotated.astype(jnp.bfloat16)
```

```python
import jax
import jax.numpy as jnp
from jax import lax
from jax.experimental import pallas as pl
from jax.experimental.pallas import tpu as pltpu
from jax.sharding import PartitionSpec as P

PANELS = 4
STEPS = 4
RING = 4
LAYERS = 8
GROUPS = 2
SLOTS = 3
CELLS = 4
NPC = 343
CPAD = 384
STACK = CELLS * CPAD
BND = 64
RIM = 2 * BND
HALF = 0.5
CENTER = 0.5
F32 = jnp.float32
BF16 = jnp.bfloat16


def dot(left, right):
    return jnp.dot(left, right, preferred_element_type=F32)


def dot_t(left, right):
    return lax.dot_general(left, right, (((1,), (1,)), ((), ())), preferred_element_type=F32)


def split(x):
    hi = x.astype(BF16)
    return hi, (x - hi.astype(F32)).astype(BF16)


def one_hot(index, shape, dim, first=0):
    places = lax.broadcasted_iota(jnp.int32, shape, dim) + first
    return jnp.where(index == places, 1.0, 0.0).astype(BF16)


def prepare_kernel(rows, scale, stiff, conn_col, conn_row, bnd_col, bnd_row, gather, scatter, finish, pack, corner):
    slot = pl.program_id(0)
    k = stiff[...]
    ghost = jnp.zeros((rows + RIM, 2 * RIM), F32)
    out = jnp.zeros((2 * RIM, rows), F32)
    for cell in range(CELLS):
        here = pl.ds(cell * CPAD, CPAD)
        factor = scale[slot, cell]
        index = conn_col[0, here, :]
        taken = one_hot(index, (CPAD, rows), 1)
        gather[0, here, :] = taken
        rim_in = one_hot(index, (CPAD, RIM), 1, rows)
        index_t = conn_row[0, :, here]
        spread = one_hot(index_t, (rows + RIM, CPAD), 0)
        scatter[0, :, here] = spread[:rows]
        column = jnp.concatenate(split(dot(k, rim_in) * factor), axis=1)
        ghost = ghost + dot(spread, column)
        row = jnp.concatenate(split(dot(spread[rows:], k) * factor), axis=0)
        out = out + dot(row, taken)
    ghost = ghost[:, :RIM] + ghost[:, RIM:]
    ghost_hi, ghost_lo = split(ghost[:rows])
    place = one_hot(bnd_row[0], (rows, RIM), 0)
    finish[0, :, 0:RIM] = ghost_hi
    finish[0, :, RIM : 2 * RIM] = ghost_lo
    finish[0, :, 2 * RIM : 3 * RIM] = place
    finish[0, :, 3 * RIM : 4 * RIM] = place
    corner_hi, corner_lo = split(ghost[rows:])
    corner[0, 0:RIM, :] = corner_hi
    corner[0, RIM : 2 * RIM, :] = corner_lo
    out_hi, out_lo = split(out[:RIM] + out[RIM:])
    pack[0, 0:RIM, :] = out_hi
    pack[0, RIM : 2 * RIM, :] = out_lo
    pack[0, 2 * RIM :, :] = one_hot(bnd_col[0], (RIM, rows), 1)


def write_rims(pack, field, rims, up, down):
    sums = dot(pack[0], field)
    terms = (sums[:RIM] + sums[RIM : 2 * RIM]).astype(BF16)
    values = sums[2 * RIM :].astype(BF16)
    rims[0] = values
    down[0, 0:BND, :] = values[:BND]
    down[0, BND:RIM, :] = terms[:BND]
    up[0, 0:BND, :] = values[BND:]
    up[0, BND:RIM, :] = terms[BND:]


def first_kernel(pack, field, corner, rims, up, down):
    write_rims(pack, field[0], rims, up, down)
    down[0, RIM : RIM + BND, :] = corner[0, 0:BND, :]
    down[0, RIM + BND : 2 * RIM, :] = corner[0, RIM : RIM + BND, :]
    up[0, RIM : RIM + BND, :] = corner[0, BND:RIM, :]
    up[0, RIM + BND : 2 * RIM, :] = corner[0, RIM + BND : 2 * RIM, :]


def local_kernel(scale, stiff, gather, scatter, field, previous, potential, base):
    slot = pl.program_id(0)
    current = field[0]
    k = stiff[...]
    blocks = []
    for cell in range(CELLS):
        local = dot(gather[0, cell * CPAD : (cell + 1) * CPAD, :], current).astype(BF16)
        product = dot(k, local) * scale[slot, cell]
        blocks.append(jnp.concatenate(split(product), axis=1))
    terms = dot(scatter[0], jnp.concatenate(blocks, axis=0))
    columns = current.shape[1]
    terms = terms[:, :columns] + terms[:, columns:]
    wide = current.astype(F32)
    applied = terms + potential[0] * wide
    base[0] = HALF * (applied - CENTER * wide) - previous[0].astype(F32)


def new_field(base, finish, rims, low, high, low2, high2, mats_low, mats_high):
    ghosts = jnp.concatenate([low[0, 0:BND, :], high[0, 0:BND, :]], axis=0)
    own = rims[0]
    to_low = jnp.concatenate([low2[0], own[:BND]], axis=0)
    to_high = jnp.concatenate([own[BND:], high2[0]], axis=0)
    back_low = low[0, BND:RIM, :].astype(F32) + dot(mats_low[0, 0:BND, :], to_low) + dot(mats_low[0, BND:RIM, :], to_low)
    back_high = high[0, BND:RIM, :].astype(F32) + dot(mats_high[0, 0:BND, :], to_high) + dot(mats_high[0, BND:RIM, :], to_high)
    back_hi, back_lo = split(jnp.concatenate([back_low, back_high], axis=0))
    right = jnp.concatenate([ghosts, ghosts, back_hi, back_lo], axis=0)
    return (base[0] + HALF * dot(finish[0], right)).astype(BF16)


def step_kernel(sel, base, finish, rims, low, high, low2, high2, mats_low, mats_high, pack, field, new_rims, up, down):
    following = new_field(base, finish, rims, low, high, low2, high2, mats_low, mats_high)
    field[0] = following
    write_rims(pack, following, new_rims, up, down)


def last_kernel(sel, base, finish, rims, low, high, low2, high2, mats_low, mats_high, field):
    field[...] = new_field(base, finish, rims, low, high, low2, high2, mats_low, mats_high)


def shape(*dims, kind=BF16):
    return jax.ShapeDtypeStruct(dims, kind)


def block(*dims):
    return pl.BlockSpec((1,) + dims, lambda s, *_: (s,) + (0,) * len(dims))


def whole(*dims):
    return pl.BlockSpec(dims, lambda s, *_: (0,) * len(dims))


SMEM = pl.BlockSpec(memory_space=pltpu.SMEM)


def params(mib):
    return pltpu.CompilerParams(vmem_limit_bytes=mib << 20)


def prepare(scale, stiff, conn, bnd, rows):
    slots = conn.shape[0]
    return pl.pallas_call(
        lambda *refs: prepare_kernel(rows, *refs),
        grid=(slots,),
        in_specs=[SMEM, whole(CPAD, CPAD), block(STACK, 1), block(1, STACK), block(RIM, 1), block(1, RIM)],
        out_specs=[block(STACK, rows), block(rows, STACK), block(rows, 4 * RIM), block(3 * RIM, rows), block(2 * RIM, RIM)],
        out_shape=[
            shape(slots, STACK, rows),
            shape(slots, rows, STACK),
            shape(slots, rows, 4 * RIM),
            shape(slots, 3 * RIM, rows),
            shape(slots, 2 * RIM, RIM),
        ],
        compiler_params=params(48),
        name="prepare",
    )(scale, stiff, conn[:, :, None], conn[:, None, :], bnd[:, :, None], bnd[:, None, :])


def first_rims(pack, field, corner):
    slots, rows, columns = field.shape
    return pl.pallas_call(
        first_kernel,
        grid=(slots,),
        in_specs=[block(3 * RIM, rows), block(rows, columns), block(2 * RIM, RIM)],
        out_specs=[block(RIM, columns), block(2 * RIM, columns), block(2 * RIM, columns)],
        out_shape=[shape(slots, RIM, columns), shape(slots, 2 * RIM, columns), shape(slots, 2 * RIM, columns)],
        compiler_params=params(32),
        name="first_rims",
    )(pack, field, corner)


def local_part(scale, stiff, gather, scatter, field, previous, potential, which):
    _, rows, columns = field.shape
    slots = len(which)
    first = which[0]

    def part(*dims):
        return pl.BlockSpec((1,) + dims, lambda s: (s + first,) + (0,) * len(dims))

    def body(scale_ref, *refs):
        local_kernel(scale_ref, *refs)

    return pl.pallas_call(
        body,
        grid=(slots,),
        in_specs=[
            SMEM,
            whole(CPAD, CPAD),
            part(STACK, rows),
            part(rows, STACK),
            part(rows, columns),
            part(rows, columns),
            part(rows, 1),
        ],
        out_specs=block(rows, columns),
        out_shape=shape(slots, rows, columns, kind=F32),
        compiler_params=params(32),
        cost_estimate=pl.CostEstimate(flops=slots * 2 * 10**9, bytes_accessed=slots * 8 * 10**6, transcendentals=0),
        name="local_part",
    )(scale[first : first + slots], stiff, gather, scatter, field, previous, potential)


def advance(sel, base, finish, rims, got, mats, pack, own):
    low, high, across = got
    mats_low, mats_high = mats
    _, rows, columns = base.shape
    first = SLOTS // 2 if own else 0
    slots = 1 if own else SLOTS

    def at(*dims):
        return pl.BlockSpec((1,) + dims, lambda s, sel: (s + first,) + (0,) * len(dims))

    def picked(which, dims, place):
        return pl.BlockSpec((1,) + dims, lambda s, sel: (sel[which, s + first],) + place)

    in_specs = [
        block(rows, columns),
        at(rows, 4 * RIM),
        at(RIM, columns),
        picked(0, (RIM, columns), (0, 0)),
        picked(1, (RIM, columns), (0, 0)),
        picked(2, (BND, columns), (1, 0)),
        picked(3, (BND, columns), (0, 0)),
        picked(4, (RIM, RIM), (1, 0)),
        picked(5, (RIM, RIM), (1, 0)),
    ]
    operands = [base, finish, rims, low, high, across, across, mats_low, mats_high]
    if own:
        out_specs = whole(rows, columns)
        out_shape = shape(rows, columns)
    else:
        in_specs.append(at(3 * RIM, rows))
        operands.append(pack)
        out_specs = [block(rows, columns)] + [block(RIM, columns)] * 3
        out_shape = [shape(slots, rows, columns)] + [shape(slots, RIM, columns)] * 3
    return pl.pallas_call(
        last_kernel if own else step_kernel,
        grid_spec=pltpu.PrefetchScalarGridSpec(num_scalar_prefetch=1, grid=(slots,), in_specs=in_specs, out_specs=out_specs),
        out_shape=out_shape,
        compiler_params=params(32),
        name="last_step" if own else "step",
    )(sel, *operands)


def place_of(device):
    return device // (RING * GROUPS), device // RING % GROUPS, device % RING


def device_at(layer, group, spot):
    return (layer % LAYERS * GROUPS + group % GROUPS) * RING + spot % RING


def shift(x, layers, groups, spots):
    pairs = []
    for device in range(LAYERS * GROUPS * RING):
        layer, group, spot = place_of(device)
        pairs.append((device, device_at(layer + layers, group + groups, spot + spots)))
    return lax.ppermute(x, "dom", pairs)


def along(x, steps):
    count = lax.axis_size("dom")
    return lax.ppermute(x, "dom", [(i, i + steps) for i in range(count) if 0 <= i + steps < count])


def turn(x, steps):
    count = lax.axis_size("orb")
    return lax.ppermute(x, "orb", [(i, (i + steps) % count) for i in range(count)])


def describe(connectivity, boundary, cell_scale, potential):
    conn = jnp.pad(connectivity, ((0, 0), (0, CPAD - connectivity.shape[1])), constant_values=-1)
    return jnp.concatenate(
        [
            conn.reshape(-1).astype(F32),
            boundary.reshape(-1).astype(F32),
            potential.astype(F32),
            cell_scale,
            jnp.zeros((RIM - CELLS,), F32),
        ]
    ).reshape(-1, RIM)


def tables(packed, rows):
    flat = packed.reshape(packed.shape[0], -1)
    conn = flat[:, :STACK].astype(jnp.int32)
    bnd = flat[:, STACK : STACK + RIM].astype(jnp.int32)
    potential = flat[:, STACK + RIM : STACK + RIM + rows]
    scale = flat[:, STACK + RIM + rows : STACK + RIM + rows + CELLS]
    return conn, bnd, potential[:, :, None], scale


def panels_of(rotation, panel_ids):
    layer, group, spot = place_of(lax.axis_index("dom"))
    mine = rotation.T
    width = mine.shape[1] // RING
    wanted = []
    for step in range(RING):
        part = lax.dynamic_slice_in_dim(mine, (spot + step) % RING * width, width, 1)
        part = shift(part, 0, 0, step) if step else part
        holder = device_at(layer, group, spot - step)
        wanted.append(jnp.where((panel_ids == holder)[:, None, None], part[None], jnp.zeros_like(part)[None]))
    held = sum(wanted[1:], wanted[0]).reshape(PANELS * mine.shape[0], width)
    width = width // GROUPS
    keep = lax.dynamic_slice_in_dim(held, group * width, width, 1)
    give = lax.dynamic_slice_in_dim(held, (1 - group) * width, width, 1)
    held = keep + shift(give, 0, 1, 0)
    for step in (1, 2, 4):
        held = held + shift(held, step, 0, 0)
    other = shift(held, 0, 1, 0)
    first = group == 0
    held = jnp.concatenate([jnp.where(first, held, other), jnp.where(first, other, held)], axis=1)
    parts = jnp.stack([held] + [shift(held, 0, 0, step) for step in range(1, RING)])
    return jnp.concatenate(
        [lax.dynamic_index_in_dim(parts, (spot - place) % RING, 0, keepdims=False) for place in range(RING)], axis=1
    )


def on_device(
    y_prev,
    y_cur,
    others,
    potential,
    stiffness,
    cell_scale,
    connectivity,
    boundary,
    rotation,
    panel_ids,
):
    rows, columns = y_cur.shape
    device = lax.axis_index("dom")
    spot = device % RING
    slot = jnp.arange(SLOTS, dtype=jnp.int32)
    below = jnp.maximum(slot - 1, 0)
    above = jnp.minimum(slot + 1, SLOTS - 1)
    sel = jnp.stack(
        [
            jnp.where(spot == 0, below, slot),
            jnp.where(spot == RING - 1, above, slot),
            jnp.where(spot < 2, below, slot),
            jnp.where(spot >= 2, above, slot),
        ]
    )

    own_tables = describe(connectivity, boundary, cell_scale, potential)
    packed = jnp.stack([along(own_tables, RING), own_tables, along(own_tables, -RING)])
    conn, bnd, pot, scale = tables(packed, rows)
    both = jnp.concatenate([y_cur, y_prev], axis=0)
    fields = jnp.stack([along(both, RING), both, along(both, -RING)])
    current, previous = fields[:, :rows], fields[:, rows:]
    stiff = jnp.pad(stiffness, ((0, CPAD - NPC), (0, CPAD - NPC)))

    gather, scatter, finish, pack, corner = prepare(scale, stiff, conn, bnd, rows)
    rims, up, down = first_rims(pack, current, corner)

    top, bottom = rims[SLOTS // 2, BND:], rims[SLOTS // 2, :BND]
    count = lax.axis_size("dom")
    pairs = [(i, i + RING + 1) for i in range(count) if i % RING == RING - 1 and i + RING + 1 < count]
    pairs += [(i, i - RING - 1) for i in range(count) if i % RING == 0 and i - RING - 1 >= 0]
    edge = lax.ppermute(jnp.where(spot == 0, bottom, top), "dom", pairs)

    mats = None
    for step in range(STEPS):
        low = shift(up, 0, 0, 1)
        high = shift(down, 0, 0, -1)
        across = shift(rims, 0, 0, 2)
        own = step == STEPS - 1
        if step == 0:
            mats = low, high
            low_first = jnp.where(spot == 0, jnp.concatenate([edge, jnp.zeros_like(edge)])[None], low[:1, :RIM])
            sel_low = low[:, :RIM]
            low_all = jnp.where(spot == 0, jnp.concatenate([low_first, sel_low[:-1]]), sel_low)
            high_last = jnp.concatenate([edge, jnp.zeros_like(edge)])[None]
            sel_high = high[:, :RIM]
            high_all = jnp.where(spot == RING - 1, jnp.concatenate([sel_high[1:], high_last]), sel_high)
            low_now, high_now = low_all, high_all
            sel_now = jnp.stack([slot, slot, sel[2], sel[3]])
            mats = (
                jnp.where(spot == 0, jnp.concatenate([low[:1], low[:-1]]), low),
                jnp.where(spot == RING - 1, jnp.concatenate([high[1:], high[-1:]]), high),
            )
        else:
            low_now, high_now, sel_now = low, high, sel
        base = local_part(scale, stiff, gather, scatter, current, previous, pot, [1] if own else [0, 1, 2])
        result = advance_call(sel_now, sel, base, finish, rims, low_now, high_now, across, mats, pack, own)
        if own:
            last = result
        else:
            previous = current
            current, rims, up, down = result

    weights_t = panels_of(rotation, panel_ids)
    block_t = weights_t[:, :columns]
    summed = lax.psum_scatter(dot_t(others, weights_t[:, columns:]), "orb", scatter_dimension=0, tiled=True)
    me = lax.axis_index("orb")
    ring = lax.axis_size("orb")
    share = rows // ring
    for step in range(ring):
        part = lax.dynamic_slice_in_dim(last, (me + step) % ring * share, share, 0)
        part = turn(part, step) if step else part
        weight = turn(block_t, step) if step else block_t
        summed = summed + dot_t(part, weight)
    return last, summed.astype(BF16)


def advance_call(sel_now, sel, base, finish, rims, low, high, across, mats, pack, own):
    slot = jnp.arange(SLOTS, dtype=jnp.int32)
    both = jnp.concatenate([sel_now, jnp.stack([slot, slot])])
    return advance(both, base, finish, rims, (low, high, across), mats, pack, own)


def solution(mesh):
    in_specs = (
        P("dom", "orb"),
        P("dom", "orb"),
        P("dom", "orb"),
        P("dom"),
        P(),
        P("dom"),
        P("dom", None),
        P("dom", None),
        P("orb", "dom"),
        P(),
    )
    out_specs = (P("dom", "orb"), P(("dom", "orb"), None))
    return jax.shard_map(
        on_device, mesh=mesh, in_specs=in_specs, out_specs=out_specs, check_vma=False
    )
```

```python
import jax
import jax.numpy as jnp
import numpy as np
from jax import lax
from jax.experimental import pallas as pl
from jax.experimental.pallas import tpu as pltpu
from jax.sharding import PartitionSpec as P

PANELS = 4
STEPS = 4
RIDE = 1
RING = 4
LAYERS = 8
GROUPS = 2
SLOTS = 3
OWN = 1
CELLS = 4
NPC = 343
CPAD = 384
STACK = CELLS * CPAD
BND = 64
RIM = 2 * BND
LANES = 128
BND_ROW = STACK // LANES
POT_ROW = BND_ROW + 1
HALF = 0.5
CENTER = 0.5
F32 = jnp.float32
BF16 = jnp.bfloat16


def dot(left, right):
    return jnp.dot(left, right, preferred_element_type=F32)


def dot_t(left, right):
    return lax.dot_general(left, right, (((1,), (1,)), ((), ())), preferred_element_type=F32)


def split(x):
    hi = x.astype(BF16)
    return hi, (x - hi.astype(F32)).astype(BF16)


def one_hot(index, shape, dim, first=0):
    places = lax.broadcasted_iota(jnp.int32, shape, dim) + first
    return jnp.where(index == places, 1.0, 0.0).astype(BF16)


def outset_kernel(*refs):
    tables, vectors, (meta, both), held, sems = refs[0:4], refs[4:6], refs[6:8], refs[8:12], refs[12:]
    copies = [pltpu.make_async_copy(table, here, sem) for table, here, sem in zip(tables, held, sems)]
    copies += [
        pltpu.make_async_copy(vector, both.at[:, place * LANES : (place + 1) * LANES], sems[4 + place])
        for place, vector in enumerate(vectors)
    ]
    for copy in copies:
        copy.start()
    for copy in copies[:4]:
        copy.wait()
    connectivity, boundary, potential, cell_scale = held
    meta[...] = jnp.full(meta.shape, -1.0, F32)
    conn = connectivity[...].astype(F32)
    per_cell = CPAD // LANES
    for cell in range(CELLS):
        for part in range(per_cell):
            first, last = part * LANES, min((part + 1) * LANES, NPC)
            meta[cell * per_cell + part : cell * per_cell + part + 1, 0 : last - first] = conn[cell : cell + 1, first:last]
    lists = boundary[...].astype(F32)
    meta[BND_ROW : BND_ROW + 1, :] = jnp.concatenate([lists[0:1], lists[1:2]], axis=1)
    meta[POT_ROW : POT_ROW + potential.shape[0], :] = potential[...].astype(F32)
    meta[POT_ROW + potential.shape[0] : POT_ROW + potential.shape[0] + 1, 0:CELLS] = cell_scale[...]
    for copy in copies[4:]:
        copy.wait()


def prepare_kernel(rows, meta, stiff, *refs):
    if len(refs) > 9:
        sel, both, _, _, direct, scatter, finish, pack, corner, potential, edge, taken, column, padded = refs
    else:
        direct, scatter, finish, pack, corner, potential, taken, column, padded = refs
        both = None
    padded[...] = jnp.zeros(padded.shape, F32)
    padded[0:NPC, 0:NPC] = stiff[...].astype(F32)
    k = padded[...].astype(BF16)
    rowed = meta[...].astype(jnp.int32)
    turned = jnp.transpose(meta[...])
    coled = turned.astype(jnp.int32)
    scales = meta[POT_ROW + rows // LANES :, :]
    per_cell = CPAD // LANES
    out_row = []
    spread_rim = []
    for cell in range(CELLS):
        factor = scales[0:1, cell : cell + 1]
        rim_in = []
        rim_out = []
        for part in range(cell * per_cell, (cell + 1) * per_cell):
            here = slice(part * LANES, (part + 1) * LANES)
            index = coled[:, part : part + 1]
            taken[here, :] = one_hot(index, (LANES, rows), 1)
            rim_in.append(one_hot(index, (LANES, RIM), 1, rows))
            index_t = rowed[part : part + 1, :]
            scatter[:, here] = one_hot(index_t, (rows, LANES), 0)
            rim_out.append(one_hot(index_t, (RIM, LANES), 0, rows))
        cells = slice(cell * CPAD, (cell + 1) * CPAD)
        column[cells, :] = jnp.concatenate(split(dot(k, jnp.concatenate(rim_in, axis=0)) * factor), axis=1)
        direct[cells, :] = dot(k, taken[cells, :]).astype(BF16)
        rim_out = jnp.concatenate(rim_out, axis=1)
        spread_rim.append(rim_out)
        out_row.append(jnp.concatenate(split(dot(rim_out, k) * factor), axis=0))
    ghost = dot(scatter[...], column[...])
    ghost_hi, ghost_lo = split(ghost[:, :RIM] + ghost[:, RIM:])
    place = one_hot(rowed[BND_ROW : BND_ROW + 1, :], (rows, RIM), 0)
    finish[:, 0:RIM] = ghost_hi
    finish[:, RIM : 2 * RIM] = ghost_lo
    finish[:, 2 * RIM : 3 * RIM] = place
    finish[:, 3 * RIM : 4 * RIM] = place
    rim = dot(jnp.concatenate(spread_rim, axis=1), column[...])
    corner_hi, corner_lo = split(rim[:, :RIM] + rim[:, RIM:])
    corner[0:RIM, :] = corner_hi
    corner[RIM : 2 * RIM, :] = corner_lo
    out = dot(jnp.concatenate(out_row, axis=1), taken[...])
    out_hi, out_lo = split(out[:RIM] + out[RIM:])
    pack[0:RIM, :] = out_hi
    pack[RIM : 2 * RIM, :] = out_lo
    pack[2 * RIM :, :] = one_hot(coled[:, BND_ROW : BND_ROW + 1], (RIM, rows), 1)
    for part in range(rows // LANES):
        values = turned[:, POT_ROW + part : POT_ROW + part + 1]
        potential[part * LANES : (part + 1) * LANES, :] = jnp.broadcast_to(values, (LANES, LANES)).astype(BF16)
    if both is not None:
        current = both[:, 0:LANES]
        values = dot(pack[2 * RIM :, :], current).astype(BF16)
        edge[...] = jnp.where(sel[4, 0] == 1, values[:BND], values[BND:])


def write_rims(slot, pack, field, rims, up, down):
    sums = dot(pack, field)
    terms = (sums[:RIM] + sums[RIM : 2 * RIM]).astype(BF16)
    values = sums[2 * RIM :].astype(BF16)
    rims[slot] = values
    down[slot, 0:BND, :] = values[:BND]
    down[slot, BND:RIM, :] = terms[:BND]
    up[slot, 0:BND, :] = values[BND:]
    up[slot, BND:RIM, :] = terms[BND:]


def first_kernel(rows, *refs):
    packs, fields, corners, (rims, up, down) = refs[0:3], refs[3:6], refs[6:9], refs[9:]
    for slot in range(SLOTS):
        write_rims(slot, packs[slot][...], fields[slot][:, 0:LANES], rims, up, down)
        corner = corners[slot]
        down[slot, RIM : RIM + BND, :] = corner[0:BND, :]
        down[slot, RIM + BND : 2 * RIM, :] = corner[RIM : RIM + BND, :]
        up[slot, RIM : RIM + BND, :] = corner[BND:RIM, :]
        up[slot, RIM + BND : 2 * RIM, :] = corner[RIM + BND : 2 * RIM, :]


def local_values(meta, direct, scatter, current, previous, potential, pieces):
    rows, columns = current.shape
    scales = meta[POT_ROW + rows // LANES :, :]
    for cell in range(CELLS):
        cells = slice(cell * CPAD, (cell + 1) * CPAD)
        product = dot(direct[cells, :], current) * scales[0:1, cell : cell + 1]
        pieces[cells, :] = jnp.concatenate(split(product), axis=1)
    terms = dot(scatter[...], pieces[...])
    terms = terms[:, :columns] + terms[:, columns:]
    wide = current.astype(F32)
    applied = terms + potential[...].astype(F32) * wide
    return HALF * (applied - CENTER * wide) - previous.astype(F32)


def local_kernel(slots, step, views, sel, *refs):
    count = len(slots)
    groups = [refs[i * count : (i + 1) * count] for i in range(6)]
    base, pieces = refs[6 * count :]
    for place, slot in enumerate(slots):
        meta, direct, scatter, field, previous, potential = (group[place] for group in groups)

        def body(place=place, meta=meta, direct=direct, scatter=scatter, field=field, previous=previous, potential=potential):
            now, before = views[place]
            base[place] = local_values(meta, direct, scatter, now(field), before(previous), potential, pieces)

        guard(sel, step, slot, body)


def guard(sel, step, slot, body):
    if slot == OWN or step == 0:
        body()
    else:
        pl.when(sel[5, slot] <= STEPS - step)(body)


def new_field(slot, sel, base, finish, rims, low, high, across, mats_low, mats_high, edge):
    from_low, from_high = low.at[sel[0, slot]], high.at[sel[1, slot]]
    mat_low, mat_high = mats_low.at[sel[0, slot]], mats_high.at[sel[1, slot]]
    below, above = from_low[0:BND, :], from_high[0:BND, :]
    if edge is not None and slot == 0:
        below = jnp.where(sel[4, 0] == 1, edge[...], below)
    if edge is not None and slot == SLOTS - 1:
        above = jnp.where(sel[4, 1] == 1, edge[...], above)
    ghosts = jnp.concatenate([below, above], axis=0)
    own = rims[slot]
    to_low = jnp.concatenate([across[sel[2, slot], BND:RIM, :], own[:BND]], axis=0)
    to_high = jnp.concatenate([own[BND:], across[sel[3, slot], 0:BND, :]], axis=0)
    back_low = from_low[BND:RIM, :].astype(F32) + sum_rims(dot(mat_low[RIM : 2 * RIM, :], to_low))
    back_high = from_high[BND:RIM, :].astype(F32) + sum_rims(dot(mat_high[RIM : 2 * RIM, :], to_high))
    back_hi, back_lo = split(jnp.concatenate([back_low, back_high], axis=0))
    right = jnp.concatenate([ghosts, ghosts, back_hi, back_lo], axis=0)
    return (base + HALF * dot(finish[...], right)).astype(BF16)


def sum_rims(x):
    return x[:BND] + x[BND:]


def step_kernel(step, sel, base_own, base_sides, *refs):
    if step == RIDE:
        refs, held = refs[:-5] + refs[-4:], refs[-5]
        for ref in refs[-3:]:
            for row in range(2):
                for col in range(2):
                    tile = held[row * RIM : (row + 1) * RIM, col * RIM : (col + 1) * RIM]
                    ref[SLOTS + 2 * row + col] = tile
    finishes, packs, refs = refs[0:3], refs[3:6], refs[6:]
    rims, low, high, across, mats_low, mats_high = refs[:6]
    refs = refs[6:]
    edge = None
    if step == 0:
        edge, refs = refs[0], refs[1:]
    field, new_rims, up, down = refs
    for slot in (0, 2, 1):

        def body(slot=slot):
            base = base_own[0] if slot == OWN else base_sides[slot // 2]
            following = new_field(slot, sel, base, finishes[slot], rims, low, high, across, mats_low, mats_high, edge)
            field[slot] = following
            write_rims(slot, packs[slot][...], following, new_rims, up, down)

        guard(sel, step, slot, body)
        if slot != OWN and step > 0:

            @pl.when(sel[5, slot] > STEPS - step)
            def _(slot=slot):
                for ref in (new_rims, up, down):
                    ref[slot] = jnp.zeros(ref.shape[1:], ref.dtype)


def others_kernel(sel, held, low, across, high, others, product, weights, panels):
    width = held.shape[1]
    for step, part in enumerate((held, low, across, high)):
        first = jnp.bitwise_and(sel[4, 2] - step, RING - 1) * width
        for row in range(2):
            for col in range(2):
                there = pl.ds(pl.multiple_of(first + col * RIM, RIM), RIM)
                rows = slice(row * RIM, (row + 1) * RIM)
                panels[rows, there] = part[rows, col * RIM : (col + 1) * RIM] if step == 0 else part[SLOTS + 2 * row + col]
    weights[...] = panels[:, 0:LANES]
    product[...] = dot_t(others[...], panels[:, LANES:])


def last_kernel(sel, base, finish, rims, low, high, across, mats_low, mats_high, weights, others_part, field, product):
    following = new_field(OWN, sel, base[0], finish, rims, low, high, across, mats_low, mats_high, None)
    field[...] = following
    product[...] = (dot_t(following, weights[...]) + others_part[...]).astype(BF16)


def shape(*dims, kind=BF16):
    return jax.ShapeDtypeStruct(dims, kind)


VMEM = pl.BlockSpec(memory_space=pltpu.VMEM)
SMEM = pl.BlockSpec(memory_space=pltpu.SMEM)


def call(kernel, name, micros, operands, out_shape, scratch=(), mib=6):
    specs = [SMEM if op.shape == (6, SLOTS) else VMEM for op in operands]
    cost = pl.CostEstimate(flops=int(micros * 1.1e9), bytes_accessed=1 << 16, transcendentals=0)
    return pl.pallas_call(
        kernel,
        in_specs=specs,
        out_specs=jax.tree.map(lambda _: VMEM, out_shape),
        out_shape=out_shape,
        scratch_shapes=scratch,
        compiler_params=pltpu.CompilerParams(vmem_limit_bytes=mib << 20),
        cost_estimate=cost,
        name=name,
    )(*operands)


def prepare(meta, stiff, rows, own=()):
    extra = [shape(BND, LANES)] if own else []
    return call(
        lambda *refs: prepare_kernel(rows, *refs),
        "prepare",
        0.1,
        [meta, stiff] + list(own),
        [
            shape(STACK, rows),
            shape(rows, STACK),
            shape(rows, 4 * RIM),
            shape(3 * RIM, rows),
            shape(2 * RIM, RIM),
            shape(rows, LANES),
        ]
        + extra,
        [pltpu.VMEM((STACK, rows), BF16), pltpu.VMEM((STACK, 2 * RIM), BF16), pltpu.VMEM((CPAD, CPAD), F32)],
        mib=10,
    )


def local_part(slots, step, sel, metas, made, fields, previous):
    rows = made[OWN][1].shape[0]
    views = [(fields[s][1], previous[s][1]) for s in slots]
    operands = [sel]
    operands += [metas[s] for s in slots]
    operands += [made[s][0] for s in slots]
    operands += [made[s][1] for s in slots]
    operands += [fields[s][0] for s in slots]
    operands += [previous[s][0] for s in slots]
    operands += [made[s][5] for s in slots]
    return call(
        lambda *refs: local_kernel(slots, step, views, *refs),
        "local_part",
        2.5 * len(slots),
        operands,
        shape(len(slots), rows, LANES, kind=F32),
        [pltpu.VMEM((STACK, 2 * LANES), BF16)],
    )


def place_of(device):
    return device // (RING * GROUPS), device // RING % GROUPS, device % RING


def device_at(layer, group, spot):
    return (layer % LAYERS * GROUPS + group % GROUPS) * RING + spot % RING


def shift(x, layers, groups, spots):
    pairs = []
    for device in range(LAYERS * GROUPS * RING):
        layer, group, spot = place_of(device)
        pairs.append((device, device_at(layer + layers, group + groups, spot + spots)))
    return lax.ppermute(x, "dom", pairs)


def along(x, steps):
    count = lax.axis_size("dom")
    return lax.ppermute(x, "dom", [(i, i + steps) for i in range(count) if 0 <= i + steps < count])


def turn(x, steps):
    count = lax.axis_size("orb")
    return lax.ppermute(x, "orb", [(i, (i + steps) % count) for i in range(count)])


def together(*values):
    return lax.optimization_barrier(values)


def panels_in_ring(rotation, panel_ids):
    layer, group, spot = place_of(lax.axis_index("dom"))
    mine = rotation.T
    width = mine.shape[1] // RING
    wanted = []
    for step in range(RING):
        part = lax.dynamic_slice_in_dim(mine, (spot + step) % RING * width, width, 1)
        part = shift(part, 0, 0, step) if step else part
        holder = device_at(layer, group, spot - step)
        wanted.append(jnp.where((panel_ids == holder)[:, None, None], part[None], jnp.zeros_like(part)[None]))
    return sum(wanted[1:], wanted[0]).reshape(PANELS * mine.shape[0], width)


def choices():
    table = np.zeros((RING, 6, SLOTS), np.int32)
    for spot in range(RING):
        for slot in range(SLOTS):
            below, above = max(slot - 1, 0), min(slot + 1, SLOTS - 1)
            table[spot, 0, slot] = below if spot == 0 else slot
            table[spot, 1, slot] = above if spot == RING - 1 else slot
            table[spot, 2, slot] = below if spot < 2 else slot
            table[spot, 3, slot] = above if spot >= 2 else slot
            table[spot, 5, slot] = (RING - spot, 0, spot + 1)[slot]
        table[spot, 4, 0] = spot == 0
        table[spot, 4, 1] = spot == RING - 1
        table[spot, 4, 2] = spot
    return table


def on_device(
    y_prev,
    y_cur,
    others,
    potential,
    stiffness,
    cell_scale,
    connectivity,
    boundary,
    rotation,
    panel_ids,
):
    rows, columns = y_cur.shape
    spot = lax.axis_index("dom") % RING
    sel = jnp.asarray(choices())[spot]

    tables = [connectivity, boundary, potential.reshape(-1, LANES), cell_scale.reshape(1, -1)]
    anywhere = pl.BlockSpec(memory_space=pltpu.HBM)
    own_meta, both = pl.pallas_call(
        outset_kernel,
        in_specs=[anywhere] * 6,
        out_specs=[VMEM, anywhere],
        out_shape=[shape(24, LANES, kind=F32), shape(rows, 2 * columns)],
        scratch_shapes=[pltpu.VMEM(t.shape, t.dtype) for t in tables] + [pltpu.SemaphoreType.DMA] * 6,
        compiler_params=pltpu.CompilerParams(vmem_limit_bytes=4 << 20),
        cost_estimate=pl.CostEstimate(flops=10**8, bytes_accessed=1 << 16, transcendentals=0),
        name="outset",
    )(*tables, y_cur, y_prev)
    metas = [along(own_meta, RING), own_meta, along(own_meta, -RING)]
    sides = [along(both, RING), both, along(both, -RING)]
    held = panels_in_ring(rotation, panel_ids)

    current = [(side, lambda ref: ref[:, 0:LANES]) for side in sides]
    previous = [(side, lambda ref: ref[:, LANES : 2 * LANES]) for side in sides]

    held, ready = together(held, own_meta)
    received = shift(held, 1, 0, 0)
    *parts, edge = prepare(ready, stiffness, rows, (sel, both, metas[0], metas[2]))
    made = [None, list(parts), None]
    made[OWN][3], held, edge = together(made[OWN][3], held, edge)
    held = held + received
    received = shift(held, 2, 0, 0)
    count = lax.axis_size("dom")
    pairs = [(i, i + RING + 1) for i in range(count) if i % RING == RING - 1 and i + RING + 1 < count]
    pairs += [(i, i - RING - 1) for i in range(count) if i % RING == 0 and i - RING - 1 >= 0]
    edge = lax.ppermute(edge, "dom", pairs)
    made[0] = list(prepare(metas[0], stiffness, rows))
    made[2] = list(prepare(metas[2], stiffness, rows))
    made[0][3], made[2][3], held = together(made[0][3], made[2][3], held)
    held = held + received

    finishes = [m[2] for m in made]
    packs = [m[3] for m in made]
    rims, up, down = call(
        lambda *refs: first_kernel(rows, *refs),
        "first_rims",
        1,
        packs + sides + [m[4] for m in made],
        [shape(SLOTS, RIM, columns), shape(SLOTS, 2 * RIM, columns), shape(SLOTS, 2 * RIM, columns)],
    )
    held, up, down, rims = together(held, up, down, rims)

    for step in range(STEPS):
        low = shift(up, 0, 0, 1)
        high = shift(down, 0, 0, -1)
        across = shift(rims, 0, 0, 2)
        if step == 0:
            mats = [low, high]
            held = held + shift(held, 4, 0, 0)
        elif step == 1:
            held = held + shift(held, 0, 1, 0)
        elif step == RIDE + 1:
            rides = [low, across, high]
        if step == STEPS - 1:
            others_part, weights = call(
                others_kernel,
                "others_part",
                1,
                [sel, held, *rides, others],
                [shape(rows, held.shape[0], kind=F32), shape(held.shape[0], columns)],
                [pltpu.VMEM((held.shape[0], RING * held.shape[1]), BF16)],
                mib=8,
            )
            base = local_part([OWN], step, sel, metas, made, current, previous)
            break
        base_sides = local_part([0, 2], step, sel, metas, made, current, previous)
        base_own = local_part([OWN], step, sel, metas, made, current, previous)
        base_sides, base_own, held = together(base_sides, base_own, held)
        operands = [sel, base_own, base_sides] + finishes + packs + [rims, low, high, across] + mats
        field, rims, up, down = call(
            lambda *refs, step=step: step_kernel(step, *refs),
            "step",
            2,
            operands + ([edge] if step == 0 else []) + ([held] if step == RIDE else []),
            [shape(SLOTS, rows, columns)] + [shape(SLOTS + (4 if step == RIDE else 0), RIM, columns)] * 3,
        )
        held, up, down, rims = together(held, up, down, rims)
        previous = current
        current = [(field, lambda ref, s=s: ref[s]) for s in range(SLOTS)]

    last, product = call(
        last_kernel,
        "last_step",
        2,
        [sel, base, finishes[OWN], rims, low, high, across] + mats + [weights, others_part],
        [shape(rows, columns), shape(rows, others_part.shape[1])],
    )
    me = lax.axis_index("orb")
    ring = lax.axis_size("orb")
    share = rows // ring
    summed = jnp.zeros((), F32)
    for step in range(ring):
        part = lax.dynamic_slice_in_dim(product, (me + step) % ring * share, share, 0)
        part = turn(part, step) if step else part
        summed = summed + part.astype(F32)
    return last, summed.astype(BF16)


def solution(mesh):
    in_specs = (
        P("dom", "orb"),
        P("dom", "orb"),
        P("dom", "orb"),
        P("dom"),
        P(),
        P("dom"),
        P("dom", None),
        P("dom", None),
        P("orb", "dom"),
        P(),
    )
    out_specs = (P("dom", "orb"), P(("dom", "orb"), None))
    return jax.shard_map(
        on_device, mesh=mesh, in_specs=in_specs, out_specs=out_specs, check_vma=False
    )
```

```python
import jax
import jax.numpy as jnp
import numpy as np
from jax import lax
from jax.experimental import pallas as pl
from jax.experimental.pallas import tpu as pltpu
from jax.sharding import PartitionSpec as P

PANELS = 4
STEPS = 4
RIDE = 1
RING = 4
LAYERS = 8
GROUPS = 2
SLOTS = 3
OWN = 1
CELLS = 4
NPC = 343
CPAD = 384
STACK = CELLS * CPAD
BND = 64
RIM = 2 * BND
LANES = 128
BND_ROW = STACK // LANES
POT_ROW = BND_ROW + 1
META = 24
HALF = 0.5
CENTER = 0.5
F32 = jnp.float32
BF16 = jnp.bfloat16


def dot(left, right):
    return jnp.dot(left, right, preferred_element_type=F32)


def dot_t(left, right):
    return lax.dot_general(left, right, (((1,), (1,)), ((), ())), preferred_element_type=F32)


def split(x):
    hi = x.astype(BF16)
    return hi, (x - hi.astype(F32)).astype(BF16)


def split_exact(x):
    hi = x.astype(BF16)
    return hi, x - hi.astype(F32)


def one_hot(index, shape, dim, first=0):
    places = lax.broadcasted_iota(jnp.int32, shape, dim) + first
    return jnp.where(index == places, 1.0, 0.0).astype(BF16)


def outset_kernel(sel, *refs):
    tables, vectors, (meta, both, edge), held, sems = refs[0:4], refs[4:6], refs[6:9], refs[9:13], refs[13:]
    copies = [pltpu.make_async_copy(table, here, sem) for table, here, sem in zip(tables, held, sems)]
    copies += [
        pltpu.make_async_copy(vector, both.at[0 : vector.shape[0], place * LANES : (place + 1) * LANES], sems[4 + place])
        for place, vector in enumerate(vectors)
    ]
    for copy in copies:
        copy.start()
    for copy in copies[:4]:
        copy.wait()
    connectivity, boundary, potential, cell_scale = held
    meta[...] = jnp.full(meta.shape, -1.0, F32)
    conn = connectivity[...].astype(F32)
    per_cell = CPAD // LANES
    for cell in range(CELLS):
        for part in range(per_cell):
            first, last = part * LANES, min((part + 1) * LANES, NPC)
            meta[cell * per_cell + part : cell * per_cell + part + 1, 0 : last - first] = conn[cell : cell + 1, first:last]
    lists = boundary[...].astype(F32)
    meta[BND_ROW : BND_ROW + 1, :] = jnp.concatenate([lists[0:1], lists[1:2]], axis=1)
    meta[POT_ROW : POT_ROW + potential.shape[0], :] = potential[...].astype(F32)
    meta[POT_ROW + potential.shape[0] : POT_ROW + potential.shape[0] + 1, 0:CELLS] = cell_scale[...]
    rows = vectors[0].shape[0]
    high, rest = split_exact(meta[...])
    middle, low = split_exact(rest)
    both[rows : rows + META, :] = jnp.concatenate([high, middle], axis=1)
    both[rows + META : rows + 2 * META, :] = jnp.concatenate([low.astype(BF16), jnp.zeros_like(high)], axis=1)
    chosen = one_hot(jnp.transpose(meta[...]).astype(jnp.int32)[:, BND_ROW : BND_ROW + 1], (RIM, rows), 1)
    for copy in copies[4:]:
        copy.wait()
    values = dot(chosen, both[0:rows, 0:LANES]).astype(BF16)
    edge[...] = jnp.where(sel[4, 0] == 1, values[:BND], values[BND:])


def prepare_kernel(rows, meta, stiff, *refs):
    if len(refs) == 9:
        direct, scatter, finish, pack, corner, potential, taken, column, padded = refs
    else:
        arrived = meta
        direct, scatter, finish, pack, corner, potential, meta, taken, column, padded = refs
        first = arrived[rows : rows + META, :].astype(F32)
        second = arrived[rows + META : rows + 2 * META, 0:LANES].astype(F32)
        meta[...] = first[:, 0:LANES] + first[:, LANES : 2 * LANES] + second
    padded[...] = jnp.zeros(padded.shape, F32)
    padded[0:NPC, 0:NPC] = stiff[...].astype(F32)
    k = padded[...].astype(BF16)
    rowed = meta[...].astype(jnp.int32)
    turned = jnp.transpose(meta[...])
    coled = turned.astype(jnp.int32)
    scales = meta[POT_ROW + rows // LANES :, :]
    per_cell = CPAD // LANES
    out_row = []
    spread_rim = []
    for cell in range(CELLS):
        factor = scales[0:1, cell : cell + 1]
        rim_in = []
        rim_out = []
        for part in range(cell * per_cell, (cell + 1) * per_cell):
            here = slice(part * LANES, (part + 1) * LANES)
            index = coled[:, part : part + 1]
            taken[here, :] = one_hot(index, (LANES, rows), 1)
            rim_in.append(one_hot(index, (LANES, RIM), 1, rows))
            index_t = rowed[part : part + 1, :]
            scatter[:, here] = one_hot(index_t, (rows, LANES), 0)
            rim_out.append(one_hot(index_t, (RIM, LANES), 0, rows))
        cells = slice(cell * CPAD, (cell + 1) * CPAD)
        column[cells, :] = jnp.concatenate(split(dot(k, jnp.concatenate(rim_in, axis=0)) * factor), axis=1)
        direct[cells, :] = dot(k, taken[cells, :]).astype(BF16)
        rim_out = jnp.concatenate(rim_out, axis=1)
        spread_rim.append(rim_out)
        out_row.append(jnp.concatenate(split(dot(rim_out, k) * factor), axis=0))
    ghost = dot(scatter[...], column[...])
    ghost_hi, ghost_lo = split(ghost[:, :RIM] + ghost[:, RIM:])
    place = one_hot(rowed[BND_ROW : BND_ROW + 1, :], (rows, RIM), 0)
    finish[:, 0:RIM] = ghost_hi
    finish[:, RIM : 2 * RIM] = ghost_lo
    finish[:, 2 * RIM : 3 * RIM] = place
    finish[:, 3 * RIM : 4 * RIM] = place
    rim = dot(jnp.concatenate(spread_rim, axis=1), column[...])
    corner_hi, corner_lo = split(rim[:, :RIM] + rim[:, RIM:])
    corner[0:RIM, :] = corner_hi
    corner[RIM : 2 * RIM, :] = corner_lo
    out = dot(jnp.concatenate(out_row, axis=1), taken[...])
    out_hi, out_lo = split(out[:RIM] + out[RIM:])
    pack[0:RIM, :] = out_hi
    pack[RIM : 2 * RIM, :] = out_lo
    pack[2 * RIM :, :] = one_hot(coled[:, BND_ROW : BND_ROW + 1], (RIM, rows), 1)
    for part in range(rows // LANES):
        values = turned[:, POT_ROW + part : POT_ROW + part + 1]
        potential[part * LANES : (part + 1) * LANES, :] = jnp.broadcast_to(values, (LANES, LANES)).astype(BF16)


def write_rims(slot, pack, field, rims, up, down):
    sums = dot(pack, field)
    terms = (sums[:RIM] + sums[RIM : 2 * RIM]).astype(BF16)
    values = sums[2 * RIM :].astype(BF16)
    rims[slot] = values
    down[slot, 0:BND, :] = values[:BND]
    down[slot, BND:RIM, :] = terms[:BND]
    up[slot, 0:BND, :] = values[BND:]
    up[slot, BND:RIM, :] = terms[BND:]


def first_kernel(rows, *refs):
    packs, fields, corners, (rims, up, down) = refs[0:3], refs[3:6], refs[6:9], refs[9:]
    for slot in range(SLOTS):
        write_rims(slot, packs[slot][...], fields[slot][0:rows, 0:LANES], rims, up, down)
        corner = corners[slot]
        down[slot, RIM : RIM + BND, :] = corner[0:BND, :]
        down[slot, RIM + BND : 2 * RIM, :] = corner[RIM : RIM + BND, :]
        up[slot, RIM : RIM + BND, :] = corner[BND:RIM, :]
        up[slot, RIM + BND : 2 * RIM, :] = corner[RIM + BND : 2 * RIM, :]


def local_values(meta, direct, scatter, current, previous, potential, pieces):
    rows, columns = current.shape
    scales = meta[POT_ROW + rows // LANES :, :]
    for cell in range(CELLS):
        cells = slice(cell * CPAD, (cell + 1) * CPAD)
        product = dot(direct[cells, :], current) * scales[0:1, cell : cell + 1]
        pieces[cells, :] = jnp.concatenate(split(product), axis=1)
    terms = dot(scatter[...], pieces[...])
    terms = terms[:, :columns] + terms[:, columns:]
    wide = current.astype(F32)
    applied = terms + potential[...].astype(F32) * wide
    return HALF * (applied - CENTER * wide) - previous.astype(F32)


def local_kernel(slots, step, views, sel, *refs):
    count = len(slots)
    groups = [refs[i * count : (i + 1) * count] for i in range(6)]
    base, pieces = refs[6 * count :]
    for place, slot in enumerate(slots):
        meta, direct, scatter, field, previous, potential = (group[place] for group in groups)

        def body(place=place, meta=meta, direct=direct, scatter=scatter, field=field, previous=previous, potential=potential):
            now, before = views[place]
            base[place] = local_values(meta, direct, scatter, now(field), before(previous), potential, pieces)

        guard(sel, step, slot, body)


def guard(sel, step, slot, body):
    if slot == OWN or step == 0:
        body()
    else:
        pl.when(sel[5, slot] <= STEPS - step)(body)


def new_field(slot, sel, base, finish, rims, low, high, across, mats_low, mats_high, edge):
    from_low, from_high = low.at[sel[0, slot]], high.at[sel[1, slot]]
    mat_low, mat_high = mats_low.at[sel[0, slot]], mats_high.at[sel[1, slot]]
    below, above = from_low[0:BND, :], from_high[0:BND, :]
    if edge is not None and slot == 0:
        below = jnp.where(sel[4, 0] == 1, edge[...], below)
    if edge is not None and slot == SLOTS - 1:
        above = jnp.where(sel[4, 1] == 1, edge[...], above)
    ghosts = jnp.concatenate([below, above], axis=0)
    own = rims[slot]
    to_low = jnp.concatenate([across[sel[2, slot], BND:RIM, :], own[:BND]], axis=0)
    to_high = jnp.concatenate([own[BND:], across[sel[3, slot], 0:BND, :]], axis=0)
    back_low = from_low[BND:RIM, :].astype(F32) + sum_rims(dot(mat_low[RIM : 2 * RIM, :], to_low))
    back_high = from_high[BND:RIM, :].astype(F32) + sum_rims(dot(mat_high[RIM : 2 * RIM, :], to_high))
    back_hi, back_lo = split(jnp.concatenate([back_low, back_high], axis=0))
    right = jnp.concatenate([ghosts, ghosts, back_hi, back_lo], axis=0)
    return (base + HALF * dot(finish[...], right)).astype(BF16)


def sum_rims(x):
    return x[:BND] + x[BND:]


def step_kernel(step, sel, base_own, base_sides, *refs):
    if step == RIDE:
        refs, held = refs[:-5] + refs[-4:], refs[-5]
        for ref in refs[-3:]:
            for row in range(2):
                for col in range(2):
                    tile = held[row * RIM : (row + 1) * RIM, col * RIM : (col + 1) * RIM]
                    ref[SLOTS + 2 * row + col] = tile
    finishes, packs, refs = refs[0:3], refs[3:6], refs[6:]
    rims, low, high, across, mats_low, mats_high = refs[:6]
    refs = refs[6:]
    edge = None
    if step == 0:
        edge, refs = refs[0], refs[1:]
    field, new_rims, up, down = refs
    for slot in (0, 2, 1):

        def body(slot=slot):
            base = base_own[0] if slot == OWN else base_sides[slot // 2]
            following = new_field(slot, sel, base, finishes[slot], rims, low, high, across, mats_low, mats_high, edge)
            field[slot] = following
            write_rims(slot, packs[slot][...], following, new_rims, up, down)

        guard(sel, step, slot, body)
        if slot != OWN and step > 0:

            @pl.when(sel[5, slot] > STEPS - step)
            def _(slot=slot):
                for ref in (new_rims, up, down):
                    ref[slot] = jnp.zeros(ref.shape[1:], ref.dtype)


def others_kernel(sel, held, low, across, high, others, product, weights, panels):
    width = held.shape[1]
    for step, part in enumerate((held, low, across, high)):
        first = jnp.bitwise_and(sel[4, 2] - step, RING - 1) * width
        for row in range(2):
            for col in range(2):
                there = pl.ds(pl.multiple_of(first + col * RIM, RIM), RIM)
                rows = slice(row * RIM, (row + 1) * RIM)
                panels[rows, there] = part[rows, col * RIM : (col + 1) * RIM] if step == 0 else part[SLOTS + 2 * row + col]
    weights[...] = panels[:, 0:LANES]
    product[...] = dot_t(others[...], panels[:, LANES:])


def last_kernel(sel, base, finish, rims, low, high, across, mats_low, mats_high, weights, others_part, field, kept, part):
    following = new_field(OWN, sel, base[0], finish, rims, low, high, across, mats_low, mats_high, None)
    field[...] = following
    share = kept.shape[1]
    for chip in range(2):
        for core, to in ((sel[6, 0], kept), (1 - sel[6, 0], part)):
            here = pl.ds(pl.multiple_of((2 * chip + core) * share, share), share)
            to[chip] = (dot_t(field[here, :], weights[...]) + others_part[here, :]).astype(to.dtype)


def shape(*dims, kind=BF16):
    return jax.ShapeDtypeStruct(dims, kind)


VMEM = pl.BlockSpec(memory_space=pltpu.VMEM)
SMEM = pl.BlockSpec(memory_space=pltpu.SMEM)


def call(kernel, name, micros, operands, out_shape, scratch=(), mib=6):
    specs = [SMEM if op.shape == (7, SLOTS) else VMEM for op in operands]
    cost = pl.CostEstimate(flops=int(micros * 1.1e9), bytes_accessed=1 << 16, transcendentals=0)
    return pl.pallas_call(
        kernel,
        in_specs=specs,
        out_specs=jax.tree.map(lambda _: VMEM, out_shape),
        out_shape=out_shape,
        scratch_shapes=scratch,
        compiler_params=pltpu.CompilerParams(vmem_limit_bytes=mib << 20),
        cost_estimate=cost,
        name=name,
    )(*operands)


def prepare(meta, stiff, rows, own=False):
    extra = [] if own else [shape(META, LANES, kind=F32)]
    return call(
        lambda *refs: prepare_kernel(rows, *refs),
        "prepare",
        0.1,
        [meta, stiff],
        [
            shape(STACK, rows),
            shape(rows, STACK),
            shape(rows, 4 * RIM),
            shape(3 * RIM, rows),
            shape(2 * RIM, RIM),
            shape(rows, LANES),
        ]
        + extra,
        [pltpu.VMEM((STACK, rows), BF16), pltpu.VMEM((STACK, 2 * RIM), BF16), pltpu.VMEM((CPAD, CPAD), F32)],
        mib=10,
    )


def local_part(slots, step, sel, metas, made, fields, previous):
    rows = made[OWN][1].shape[0]
    views = [(fields[s][1], previous[s][1]) for s in slots]
    operands = [sel]
    operands += [metas[s] for s in slots]
    operands += [made[s][0] for s in slots]
    operands += [made[s][1] for s in slots]
    operands += [fields[s][0] for s in slots]
    operands += [previous[s][0] for s in slots]
    operands += [made[s][5] for s in slots]
    return call(
        lambda *refs: local_kernel(slots, step, views, *refs),
        "local_part",
        0.3 * len(slots),
        operands,
        shape(len(slots), rows, LANES, kind=F32),
        [pltpu.VMEM((STACK, 2 * LANES), BF16)],
    )


def place_of(device):
    return device // (RING * GROUPS), device // RING % GROUPS, device % RING


def device_at(layer, group, spot):
    return (layer % LAYERS * GROUPS + group % GROUPS) * RING + spot % RING


def shift(x, layers, groups, spots):
    pairs = []
    for device in range(LAYERS * GROUPS * RING):
        layer, group, spot = place_of(device)
        pairs.append((device, device_at(layer + layers, group + groups, spot + spots)))
    return lax.ppermute(x, "dom", pairs)


def along(x, steps):
    count = lax.axis_size("dom")
    return lax.ppermute(x, "dom", [(i, i + steps) for i in range(count) if 0 <= i + steps < count])


def turn(x, steps):
    count = lax.axis_size("orb")
    return lax.ppermute(x, "orb", [(i, (i + steps) % count) for i in range(count)])


def together(*values):
    return lax.optimization_barrier(values)


def panels_in_ring(rotation, panel_ids):
    layer, group, spot = place_of(lax.axis_index("dom"))
    mine = rotation.T
    width = mine.shape[1] // RING
    wanted = []
    for step in range(RING):
        part = lax.dynamic_slice_in_dim(mine, (spot + step) % RING * width, width, 1)
        part = shift(part, 0, 0, step) if step else part
        holder = device_at(layer, group, spot - step)
        wanted.append(jnp.where((panel_ids == holder)[:, None, None], part[None], jnp.zeros_like(part)[None]))
    return sum(wanted[1:], wanted[0]).reshape(PANELS * mine.shape[0], width)


def choices():
    table = np.zeros((RING, 2, 7, SLOTS), np.int32)
    for spot in range(RING):
        for slot in range(SLOTS):
            below, above = max(slot - 1, 0), min(slot + 1, SLOTS - 1)
            table[spot, :, 0, slot] = below if spot == 0 else slot
            table[spot, :, 1, slot] = above if spot == RING - 1 else slot
            table[spot, :, 2, slot] = below if spot < 2 else slot
            table[spot, :, 3, slot] = above if spot >= 2 else slot
            table[spot, :, 5, slot] = (RING - spot, 0, spot + 1)[slot]
        table[spot, :, 4, 0] = spot == 0
        table[spot, :, 4, 1] = spot == RING - 1
        table[spot, :, 4, 2] = spot
        table[spot, 1, 6, 0] = 1
    return table


def on_device(
    y_prev,
    y_cur,
    others,
    potential,
    stiffness,
    cell_scale,
    connectivity,
    boundary,
    rotation,
    panel_ids,
):
    rows, columns = y_cur.shape
    spot = lax.axis_index("dom") % RING
    sel = jnp.asarray(choices())[spot, lax.axis_index("orb") % 2]

    tables = [connectivity, boundary, potential.reshape(-1, LANES), cell_scale.reshape(1, -1)]
    sent_rows = rows + 2 * META
    own_meta, both, edge = pl.pallas_call(
        outset_kernel,
        grid=(1,),
        in_specs=[SMEM] + [pl.BlockSpec(memory_space=pl.ANY)] * 6,
        out_specs=[pl.BlockSpec(dims, lambda i: (0, 0)) for dims in ((META, LANES), (sent_rows, 2 * LANES), (BND, LANES))],
        out_shape=[shape(META, LANES, kind=F32), shape(sent_rows, 2 * columns), shape(BND, columns)],
        scratch_shapes=[pltpu.VMEM(t.shape, t.dtype) for t in tables] + [pltpu.SemaphoreType.DMA] * 6,
        compiler_params=pltpu.CompilerParams(vmem_limit_bytes=60 << 20),
        cost_estimate=pl.CostEstimate(flops=10**8, bytes_accessed=1 << 16, transcendentals=0),
        name="outset",
    )(sel, *tables, y_cur, y_prev)
    sides = [along(both, RING), both, along(both, -RING)]
    held = panels_in_ring(rotation, panel_ids)

    current = [(side, lambda ref: ref[0:rows, 0:LANES]) for side in sides]
    previous = [(side, lambda ref: ref[0:rows, LANES : 2 * LANES]) for side in sides]

    received = shift(held, 1, 0, 0)
    parts = prepare(own_meta, stiffness, rows, own=True)
    made = [None, list(parts), None]
    made[OWN][3], held = together(made[OWN][3], held)
    held = held + received
    received = shift(held, 2, 0, 0)
    count = lax.axis_size("dom")
    pairs = [(i, i + RING + 1) for i in range(count) if i % RING == RING - 1 and i + RING + 1 < count]
    pairs += [(i, i - RING - 1) for i in range(count) if i % RING == 0 and i - RING - 1 >= 0]
    edge = lax.ppermute(edge, "dom", pairs)
    made[0] = list(prepare(sides[0], stiffness, rows))
    made[2] = list(prepare(sides[2], stiffness, rows))
    metas = [made[0][6], own_meta, made[2][6]]
    made[0][3], made[2][3], held = together(made[0][3], made[2][3], held)
    held = held + received

    finishes = [m[2] for m in made]
    packs = [m[3] for m in made]
    rims, up, down = call(
        lambda *refs: first_kernel(rows, *refs),
        "first_rims",
        1,
        packs + sides + [m[4] for m in made],
        [shape(SLOTS, RIM, columns), shape(SLOTS, 2 * RIM, columns), shape(SLOTS, 2 * RIM, columns)],
    )
    held, up, down, rims, own_both = together(held, up, down, rims, both)
    current[OWN] = (own_both, current[OWN][1])
    previous[OWN] = (own_both, previous[OWN][1])

    for step in range(STEPS):
        low = shift(up, 0, 0, 1)
        high = shift(down, 0, 0, -1)
        across = shift(rims, 0, 0, 2)
        if step == 0:
            mats = [low, high]
            held = held + shift(held, 4, 0, 0)
        elif step == 1:
            held = held + shift(held, 0, 1, 0)
        elif step == RIDE + 1:
            rides = [low, across, high]
        if step == STEPS - 1:
            others_part, weights = call(
                others_kernel,
                "others_part",
                0.2,
                [sel, held, *rides, others],
                [shape(rows, held.shape[0], kind=F32), shape(held.shape[0], columns)],
                [pltpu.VMEM((held.shape[0], RING * held.shape[1]), BF16)],
                mib=8,
            )
            base = local_part([OWN], step, sel, metas, made, current, previous)
            break
        base_sides = local_part([0, 2], step, sel, metas, made, current, previous)
        base_own = local_part([OWN], step, sel, metas, made, current, previous)
        base_sides, base_own, held = together(base_sides, base_own, held)
        operands = [sel, base_own, base_sides] + finishes + packs + [rims, low, high, across] + mats
        field, rims, up, down = call(
            lambda *refs, step=step: step_kernel(step, *refs),
            "step",
            2,
            operands + ([edge] if step == 0 else []) + ([held] if step == RIDE else []),
            [shape(SLOTS, rows, columns)] + [shape(SLOTS + (4 if step == RIDE else 0), RIM, columns)] * 3,
        )
        held, up, down, rims = together(held, up, down, rims)
        previous = current
        current = [(field, lambda ref, s=s: ref[s]) for s in range(SLOTS)]

    share = rows // lax.axis_size("orb")
    last, kept, part = call(
        last_kernel,
        "last_step",
        2,
        [sel, base, finishes[OWN], rims, low, high, across] + mats + [weights, others_part],
        [
            shape(rows, columns),
            shape(2, share, others_part.shape[1], kind=F32),
            shape(2, share, others_part.shape[1]),
        ],
    )
    me = lax.axis_index("orb")
    chip = me // 2
    part = kept + lax.ppermute(part, "orb", [(i, i ^ 1) for i in range(4)]).astype(F32)
    other = lax.dynamic_index_in_dim(part, 1 - chip, 0, keepdims=False).astype(BF16)
    summed = lax.dynamic_index_in_dim(part, chip, 0, keepdims=False)
    summed = summed + lax.ppermute(other, "orb", [(i, i ^ 2) for i in range(4)]).astype(F32)
    return last, summed.astype(BF16)


def solution(mesh):
    in_specs = (
        P("dom", "orb"),
        P("dom", "orb"),
        P("dom", "orb"),
        P("dom"),
        P(),
        P("dom"),
        P("dom", None),
        P("dom", None),
        P("orb", "dom"),
        P(),
    )
    out_specs = (P("dom", "orb"), P(("dom", "orb"), None))
    return jax.shard_map(
        on_device, mesh=mesh, in_specs=in_specs, out_specs=out_specs, check_vma=False
    )
```

```python
import jax
import jax.numpy as jnp
import numpy as np
from jax import lax
from jax.experimental import pallas as pl
from jax.experimental.pallas import tpu as pltpu
from jax.sharding import PartitionSpec as P

PANELS = 4
STEPS = 4
RIDE = 1
RING = 4
LAYERS = 8
GROUPS = 2
SLOTS = 3
OWN = 1
CELLS = 4
NPC = 343
CPAD = 384
STACK = CELLS * CPAD
BND = 64
RIM = 2 * BND
LANES = 128
BND_ROW = STACK // LANES
POT_ROW = BND_ROW + 1
META = 24
HALF = 0.5
CENTER = 0.5
F32 = jnp.float32
BF16 = jnp.bfloat16


def dot(left, right):
    return jnp.dot(left, right, preferred_element_type=F32)


def dot_t(left, right):
    return lax.dot_general(left, right, (((1,), (1,)), ((), ())), preferred_element_type=F32)


def split(x):
    hi = x.astype(BF16)
    return hi, (x - hi.astype(F32)).astype(BF16)


def split_exact(x):
    hi = x.astype(BF16)
    return hi, x - hi.astype(F32)


def one_hot(index, shape, dim, first=0):
    places = lax.broadcasted_iota(jnp.int32, shape, dim) + first
    return jnp.where(index == places, 1.0, 0.0).astype(BF16)


def outset_kernel(sel, *refs):
    tables, vectors, (meta, both, edge), held, sems = refs[0:4], refs[4:6], refs[6:9], refs[9:13], refs[13:]
    copies = [pltpu.make_async_copy(table, here, sem) for table, here, sem in zip(tables, held, sems)]
    copies += [
        pltpu.make_async_copy(vector, both.at[0 : vector.shape[0], place * LANES : (place + 1) * LANES], sems[4 + place])
        for place, vector in enumerate(vectors)
    ]
    for copy in copies:
        copy.start()
    for copy in copies[:4]:
        copy.wait()
    connectivity, boundary, potential, cell_scale = held
    meta[...] = jnp.full(meta.shape, -1.0, F32)
    conn = connectivity[...].astype(F32)
    per_cell = CPAD // LANES
    for cell in range(CELLS):
        for part in range(per_cell):
            first, last = part * LANES, min((part + 1) * LANES, NPC)
            meta[cell * per_cell + part : cell * per_cell + part + 1, 0 : last - first] = conn[cell : cell + 1, first:last]
    lists = boundary[...].astype(F32)
    meta[BND_ROW : BND_ROW + 1, :] = jnp.concatenate([lists[0:1], lists[1:2]], axis=1)
    meta[POT_ROW : POT_ROW + potential.shape[0], :] = potential[...].astype(F32)
    meta[POT_ROW + potential.shape[0] : POT_ROW + potential.shape[0] + 1, 0:CELLS] = cell_scale[...]
    rows = vectors[0].shape[0]
    high, rest = split_exact(meta[...])
    middle, low = split_exact(rest)
    both[rows : rows + META, :] = jnp.concatenate([high, middle], axis=1)
    both[rows + META : rows + 2 * META, :] = jnp.concatenate([low.astype(BF16), jnp.zeros_like(high)], axis=1)
    chosen = one_hot(jnp.transpose(meta[...]).astype(jnp.int32)[:, BND_ROW : BND_ROW + 1], (RIM, rows), 1)
    for copy in copies[4:]:
        copy.wait()
    values = dot(chosen, both[0:rows, 0:LANES]).astype(BF16)
    edge[...] = jnp.where(sel[4, 0] == 1, values[:BND], values[BND:])


def prepare_kernel(rows, meta, stiff, *refs):
    if len(refs) == 10:
        direct, scatter, finish, pack, corner, potential, ready, taken, column, padded = refs
        padded[...] = jnp.zeros(padded.shape, F32)
        padded[0:NPC, 0:NPC] = stiff[...].astype(F32)
        ready[...] = padded[...].astype(BF16)
        stiff = ready
    else:
        arrived = meta
        direct, scatter, finish, pack, corner, potential, meta, taken, column = refs
        first = arrived[rows : rows + META, :].astype(F32)
        second = arrived[rows + META : rows + 2 * META, 0:LANES].astype(F32)
        meta[...] = first[:, 0:LANES] + first[:, LANES : 2 * LANES] + second
    k = stiff[...]
    rowed = meta[...].astype(jnp.int32)
    turned = jnp.transpose(meta[...])
    coled = turned.astype(jnp.int32)
    scales = meta[POT_ROW + rows // LANES :, :]
    per_cell = CPAD // LANES
    out_row = []
    spread_rim = []
    for cell in range(CELLS):
        factor = scales[0:1, cell : cell + 1]
        rim_in = []
        rim_out = []
        for part in range(cell * per_cell, (cell + 1) * per_cell):
            here = slice(part * LANES, (part + 1) * LANES)
            index = coled[:, part : part + 1]
            taken[here, :] = one_hot(index, (LANES, rows), 1)
            rim_in.append(one_hot(index, (LANES, RIM), 1, rows))
            index_t = rowed[part : part + 1, :]
            scatter[:, here] = one_hot(index_t, (rows, LANES), 0)
            rim_out.append(one_hot(index_t, (RIM, LANES), 0, rows))
        cells = slice(cell * CPAD, (cell + 1) * CPAD)
        column[cells, :] = jnp.concatenate(split(dot(k, jnp.concatenate(rim_in, axis=0)) * factor), axis=1)
        direct[cells, :] = dot(k, taken[cells, :]).astype(BF16)
        rim_out = jnp.concatenate(rim_out, axis=1)
        spread_rim.append(rim_out)
        out_row.append(jnp.concatenate(split(dot(rim_out, k) * factor), axis=0))
    ghost = dot(scatter[...], column[...])
    ghost_hi, ghost_lo = split(ghost[:, :RIM] + ghost[:, RIM:])
    place = one_hot(rowed[BND_ROW : BND_ROW + 1, :], (rows, RIM), 0)
    finish[:, 0:RIM] = ghost_hi
    finish[:, RIM : 2 * RIM] = ghost_lo
    finish[:, 2 * RIM : 3 * RIM] = place
    finish[:, 3 * RIM : 4 * RIM] = place
    rim = dot(jnp.concatenate(spread_rim, axis=1), column[...])
    corner_hi, corner_lo = split(rim[:, :RIM] + rim[:, RIM:])
    corner[0:RIM, :] = corner_hi
    corner[RIM : 2 * RIM, :] = corner_lo
    out = dot(jnp.concatenate(out_row, axis=1), taken[...])
    out_hi, out_lo = split(out[:RIM] + out[RIM:])
    pack[0:RIM, :] = out_hi
    pack[RIM : 2 * RIM, :] = out_lo
    pack[2 * RIM :, :] = one_hot(coled[:, BND_ROW : BND_ROW + 1], (RIM, rows), 1)
    for part in range(rows // LANES):
        values = turned[:, POT_ROW + part : POT_ROW + part + 1]
        potential[part * LANES : (part + 1) * LANES, :] = jnp.broadcast_to(values, (LANES, LANES)).astype(BF16)


def write_rims(slot, pack, field, rims, up, down):
    sums = dot(pack, field)
    terms = (sums[:RIM] + sums[RIM : 2 * RIM]).astype(BF16)
    values = sums[2 * RIM :].astype(BF16)
    rims[slot] = values
    down[slot, 0:BND, :] = values[:BND]
    down[slot, BND:RIM, :] = terms[:BND]
    up[slot, 0:BND, :] = values[BND:]
    up[slot, BND:RIM, :] = terms[BND:]


def first_kernel(rows, *refs):
    packs, fields, corners, (rims, up, down) = refs[0:3], refs[3:6], refs[6:9], refs[9:]
    for slot in range(SLOTS):
        write_rims(slot, packs[slot][...], fields[slot][0:rows, 0:LANES], rims, up, down)
        corner = corners[slot]
        down[slot, RIM : RIM + BND, :] = corner[0:BND, :]
        down[slot, RIM + BND : 2 * RIM, :] = corner[RIM : RIM + BND, :]
        up[slot, RIM : RIM + BND, :] = corner[BND:RIM, :]
        up[slot, RIM + BND : 2 * RIM, :] = corner[RIM + BND : 2 * RIM, :]


def local_values(meta, direct, scatter, current, previous, potential, pieces):
    rows, columns = current.shape
    scales = meta[POT_ROW + rows // LANES :, :]
    for cell in range(CELLS):
        cells = slice(cell * CPAD, (cell + 1) * CPAD)
        product = dot(direct[cells, :], current) * scales[0:1, cell : cell + 1]
        pieces[cells, :] = jnp.concatenate(split(product), axis=1)
    terms = dot(scatter[...], pieces[...])
    terms = terms[:, :columns] + terms[:, columns:]
    wide = current.astype(F32)
    applied = terms + potential[...].astype(F32) * wide
    return HALF * (applied - CENTER * wide) - previous.astype(F32)


def local_kernel(slots, step, views, sel, *refs):
    count = len(slots)
    groups = [refs[i * count : (i + 1) * count] for i in range(6)]
    base, pieces = refs[6 * count :]
    for place, slot in enumerate(slots):
        meta, direct, scatter, field, previous, potential = (group[place] for group in groups)

        def body(place=place, meta=meta, direct=direct, scatter=scatter, field=field, previous=previous, potential=potential):
            now, before = views[place]
            base[place] = local_values(meta, direct, scatter, now(field), before(previous), potential, pieces)

        guard(sel, step, slot, body)


def guard(sel, step, slot, body):
    if slot == OWN or step == 0:
        body()
    else:
        pl.when(sel[5, slot] <= STEPS - step)(body)


def new_field(slot, sel, base, finish, rims, low, high, across, mats_low, mats_high, edge):
    from_low, from_high = low.at[sel[0, slot]], high.at[sel[1, slot]]
    mat_low, mat_high = mats_low.at[sel[0, slot]], mats_high.at[sel[1, slot]]
    below, above = from_low[0:BND, :], from_high[0:BND, :]
    if edge is not None and slot == 0:
        below = jnp.where(sel[4, 0] == 1, edge[...], below)
    if edge is not None and slot == SLOTS - 1:
        above = jnp.where(sel[4, 1] == 1, edge[...], above)
    ghosts = jnp.concatenate([below, above], axis=0)
    own = rims[slot]
    to_low = jnp.concatenate([across[sel[2, slot], BND:RIM, :], own[:BND]], axis=0)
    to_high = jnp.concatenate([own[BND:], across[sel[3, slot], 0:BND, :]], axis=0)
    back_low = from_low[BND:RIM, :].astype(F32) + sum_rims(dot(mat_low[RIM : 2 * RIM, :], to_low))
    back_high = from_high[BND:RIM, :].astype(F32) + sum_rims(dot(mat_high[RIM : 2 * RIM, :], to_high))
    back_hi, back_lo = split(jnp.concatenate([back_low, back_high], axis=0))
    right = jnp.concatenate([ghosts, ghosts, back_hi, back_lo], axis=0)
    return (base + HALF * dot(finish[...], right)).astype(BF16)


def sum_rims(x):
    return x[:BND] + x[BND:]


def step_kernel(step, sel, base_own, base_sides, *refs):
    if step == RIDE:
        refs, held = refs[:-5] + refs[-4:], refs[-5]
        for ref in refs[-3:]:
            for row in range(2):
                for col in range(2):
                    tile = held[row * RIM : (row + 1) * RIM, col * RIM : (col + 1) * RIM]
                    ref[SLOTS + 2 * row + col] = tile
    finishes, packs, refs = refs[0:3], refs[3:6], refs[6:]
    rims, low, high, across, mats_low, mats_high = refs[:6]
    refs = refs[6:]
    edge = None
    if step == 0:
        edge, refs = refs[0], refs[1:]
    field, new_rims, up, down = refs
    for slot in (0, 2, 1):

        def body(slot=slot):
            base = base_own[0] if slot == OWN else base_sides[slot // 2]
            following = new_field(slot, sel, base, finishes[slot], rims, low, high, across, mats_low, mats_high, edge)
            field[slot] = following
            write_rims(slot, packs[slot][...], following, new_rims, up, down)

        guard(sel, step, slot, body)
        if slot != OWN and step > 0:

            @pl.when(sel[5, slot] > STEPS - step)
            def _(slot=slot):
                for ref in (new_rims, up, down):
                    ref[slot] = jnp.zeros(ref.shape[1:], ref.dtype)


def others_kernel(sel, held, low, across, high, others, product, weights, panels):
    width = held.shape[1]
    for step, part in enumerate((held, low, across, high)):
        first = jnp.bitwise_and(sel[4, 2] - step, RING - 1) * width
        for row in range(2):
            for col in range(2):
                there = pl.ds(pl.multiple_of(first + col * RIM, RIM), RIM)
                rows = slice(row * RIM, (row + 1) * RIM)
                panels[rows, there] = part[rows, col * RIM : (col + 1) * RIM] if step == 0 else part[SLOTS + 2 * row + col]
    weights[...] = panels[:, 0:LANES]
    product[...] = dot_t(others[...], panels[:, LANES:])


def last_kernel(sel, base, finish, rims, low, high, across, mats_low, mats_high, weights, others_part, field, kept, part):
    following = new_field(OWN, sel, base[0], finish, rims, low, high, across, mats_low, mats_high, None)
    field[...] = following
    share = kept.shape[1]
    for chip in range(2):
        for core, to in ((sel[6, 0], kept), (1 - sel[6, 0], part)):
            here = pl.ds(pl.multiple_of((2 * chip + core) * share, share), share)
            to[chip] = (dot_t(field[here, :], weights[...]) + others_part[here, :]).astype(to.dtype)


def shape(*dims, kind=BF16):
    return jax.ShapeDtypeStruct(dims, kind)


VMEM = pl.BlockSpec(memory_space=pltpu.VMEM)
SMEM = pl.BlockSpec(memory_space=pltpu.SMEM)


def call(kernel, name, micros, operands, out_shape, scratch=(), mib=6):
    specs = [SMEM if op.shape == (7, SLOTS) else VMEM for op in operands]
    cost = pl.CostEstimate(flops=int(micros * 1.1e9), bytes_accessed=1 << 16, transcendentals=0)
    return pl.pallas_call(
        kernel,
        in_specs=specs,
        out_specs=jax.tree.map(lambda _: VMEM, out_shape),
        out_shape=out_shape,
        scratch_shapes=scratch,
        compiler_params=pltpu.CompilerParams(vmem_limit_bytes=mib << 20),
        cost_estimate=cost,
        name=name,
    )(*operands)


def prepare(meta, stiff, rows, own=False):
    extra = [shape(CPAD, CPAD)] if own else [shape(META, LANES, kind=F32)]
    return call(
        lambda *refs: prepare_kernel(rows, *refs),
        "prepare",
        0.1,
        [meta, stiff],
        [
            shape(STACK, rows),
            shape(rows, STACK),
            shape(rows, 4 * RIM),
            shape(3 * RIM, rows),
            shape(2 * RIM, RIM),
            shape(rows, LANES),
        ]
        + extra,
        [pltpu.VMEM((STACK, rows), BF16), pltpu.VMEM((STACK, 2 * RIM), BF16)]
        + ([pltpu.VMEM((CPAD, CPAD), F32)] if own else []),
        mib=10,
    )


def local_part(slots, step, sel, metas, made, fields, previous):
    rows = made[OWN][1].shape[0]
    views = [(fields[s][1], previous[s][1]) for s in slots]
    operands = [sel]
    operands += [metas[s] for s in slots]
    operands += [made[s][0] for s in slots]
    operands += [made[s][1] for s in slots]
    operands += [fields[s][0] for s in slots]
    operands += [previous[s][0] for s in slots]
    operands += [made[s][5] for s in slots]
    return call(
        lambda *refs: local_kernel(slots, step, views, *refs),
        "local_part",
        0.3 * len(slots),
        operands,
        shape(len(slots), rows, LANES, kind=F32),
        [pltpu.VMEM((STACK, 2 * LANES), BF16)],
    )


def place_of(device):
    return device // (RING * GROUPS), device // RING % GROUPS, device % RING


def device_at(layer, group, spot):
    return (layer % LAYERS * GROUPS + group % GROUPS) * RING + spot % RING


def shift(x, layers, groups, spots):
    pairs = []
    for device in range(LAYERS * GROUPS * RING):
        layer, group, spot = place_of(device)
        pairs.append((device, device_at(layer + layers, group + groups, spot + spots)))
    return lax.ppermute(x, "dom", pairs)


def swap(x, layers, spots):
    pairs = []
    for device in range(LAYERS * GROUPS * RING):
        layer, group, spot = place_of(device)
        pairs.append((device, device_at(layer ^ layers, group, spot ^ spots)))
    return lax.ppermute(x, "dom", pairs)


def along(x, steps):
    count = lax.axis_size("dom")
    return lax.ppermute(x, "dom", [(i, i + steps) for i in range(count) if 0 <= i + steps < count])


def turn(x, steps):
    count = lax.axis_size("orb")
    return lax.ppermute(x, "orb", [(i, (i + steps) % count) for i in range(count)])


def together(*values):
    return lax.optimization_barrier(values)


def panels_in_ring(rotation, panel_ids):
    layer, group, spot = place_of(lax.axis_index("dom"))
    mine = rotation.T
    width = mine.shape[1] // RING
    wanted = []
    for step in range(RING):
        part = lax.dynamic_slice_in_dim(mine, (spot ^ step) * width, width, 1)
        part = swap(part, 0, step) if step else part
        holder = device_at(layer, group, spot ^ step)
        wanted.append(jnp.where((panel_ids == holder)[:, None, None], part[None], jnp.zeros_like(part)[None]))
    return sum(wanted[1:], wanted[0]).reshape(PANELS * mine.shape[0], width)


def choices():
    table = np.zeros((RING, 2, 7, SLOTS), np.int32)
    for spot in range(RING):
        for slot in range(SLOTS):
            below, above = max(slot - 1, 0), min(slot + 1, SLOTS - 1)
            table[spot, :, 0, slot] = below if spot == 0 else slot
            table[spot, :, 1, slot] = above if spot == RING - 1 else slot
            table[spot, :, 2, slot] = below if spot < 2 else slot
            table[spot, :, 3, slot] = above if spot >= 2 else slot
            table[spot, :, 5, slot] = (RING - spot, 0, spot + 1)[slot]
        table[spot, :, 4, 0] = spot == 0
        table[spot, :, 4, 1] = spot == RING - 1
        table[spot, :, 4, 2] = spot
        table[spot, 1, 6, 0] = 1
    return table


def on_device(
    y_prev,
    y_cur,
    others,
    potential,
    stiffness,
    cell_scale,
    connectivity,
    boundary,
    rotation,
    panel_ids,
):
    rows, columns = y_cur.shape
    spot = lax.axis_index("dom") % RING
    sel = jnp.asarray(choices())[spot, lax.axis_index("orb") % 2]

    tables = [connectivity, boundary, potential.reshape(-1, LANES), cell_scale.reshape(1, -1)]
    sent_rows = rows + 2 * META
    own_meta, both, edge = pl.pallas_call(
        outset_kernel,
        grid=(1,),
        in_specs=[SMEM] + [pl.BlockSpec(memory_space=pl.ANY)] * 6,
        out_specs=[pl.BlockSpec(dims, lambda i: (0, 0)) for dims in ((META, LANES), (sent_rows, 2 * LANES), (BND, LANES))],
        out_shape=[shape(META, LANES, kind=F32), shape(sent_rows, 2 * columns), shape(BND, columns)],
        scratch_shapes=[pltpu.VMEM(t.shape, t.dtype) for t in tables] + [pltpu.SemaphoreType.DMA] * 6,
        compiler_params=pltpu.CompilerParams(vmem_limit_bytes=60 << 20),
        cost_estimate=pl.CostEstimate(flops=10**8, bytes_accessed=1 << 16, transcendentals=0),
        name="outset",
    )(sel, *tables, y_cur, y_prev)
    sides = [along(both, RING), both, along(both, -RING)]
    held = panels_in_ring(rotation, panel_ids)

    current = [(side, lambda ref: ref[0:rows, 0:LANES]) for side in sides]
    previous = [(side, lambda ref: ref[0:rows, LANES : 2 * LANES]) for side in sides]

    received = swap(held, 1, 0)
    *parts, stiff = prepare(own_meta, stiffness, rows, own=True)
    made = [None, list(parts), None]
    made[OWN][3], held = together(made[OWN][3], held)
    held = held + received
    received = swap(held, 2, 0)
    count = lax.axis_size("dom")
    pairs = [(i, i + RING + 1) for i in range(count) if i % RING == RING - 1 and i + RING + 1 < count]
    pairs += [(i, i - RING - 1) for i in range(count) if i % RING == 0 and i - RING - 1 >= 0]
    edge = lax.ppermute(edge, "dom", pairs)
    made[0] = list(prepare(sides[0], stiff, rows))
    made[2] = list(prepare(sides[2], stiff, rows))
    metas = [made[0][6], own_meta, made[2][6]]
    made[0][3], made[2][3], held = together(made[0][3], made[2][3], held)
    held = held + received

    finishes = [m[2] for m in made]
    packs = [m[3] for m in made]
    rims, up, down = call(
        lambda *refs: first_kernel(rows, *refs),
        "first_rims",
        1,
        packs + sides + [m[4] for m in made],
        [shape(SLOTS, RIM, columns), shape(SLOTS, 2 * RIM, columns), shape(SLOTS, 2 * RIM, columns)],
    )
    held, up, down, rims, own_both = together(held, up, down, rims, both)
    current[OWN] = (own_both, current[OWN][1])
    previous[OWN] = (own_both, previous[OWN][1])

    for step in range(STEPS):
        low = shift(up, 0, 0, 1)
        high = shift(down, 0, 0, -1)
        across = shift(rims, 0, 0, 2)
        if step == 0:
            mats = [low, high]
            held = held + swap(held, 4, 0)
        elif step == 1:
            held = held + shift(held, 0, 1, 0)
        elif step == RIDE + 1:
            rides = [low, across, high]
        if step == STEPS - 1:
            others_part, weights = call(
                others_kernel,
                "others_part",
                0.2,
                [sel, held, *rides, others],
                [shape(rows, held.shape[0], kind=F32), shape(held.shape[0], columns)],
                [pltpu.VMEM((held.shape[0], RING * held.shape[1]), BF16)],
                mib=8,
            )
            base = local_part([OWN], step, sel, metas, made, current, previous)
            break
        base_sides = local_part([0, 2], step, sel, metas, made, current, previous)
        base_own = local_part([OWN], step, sel, metas, made, current, previous)
        base_sides, base_own, held = together(base_sides, base_own, held)
        operands = [sel, base_own, base_sides] + finishes + packs + [rims, low, high, across] + mats
        field, rims, up, down = call(
            lambda *refs, step=step: step_kernel(step, *refs),
            "step",
            2,
            operands + ([edge] if step == 0 else []) + ([held] if step == RIDE else []),
            [shape(SLOTS, rows, columns)] + [shape(SLOTS + (4 if step == RIDE else 0), RIM, columns)] * 3,
        )
        held, up, down, rims = together(held, up, down, rims)
        previous = current
        current = [(field, lambda ref, s=s: ref[s]) for s in range(SLOTS)]

    share = rows // lax.axis_size("orb")
    last, kept, part = call(
        last_kernel,
        "last_step",
        2,
        [sel, base, finishes[OWN], rims, low, high, across] + mats + [weights, others_part],
        [
            shape(rows, columns),
            shape(2, share, others_part.shape[1], kind=F32),
            shape(2, share, others_part.shape[1]),
        ],
    )
    me = lax.axis_index("orb")
    chip = me // 2
    part = kept + lax.ppermute(part, "orb", [(i, i ^ 1) for i in range(4)]).astype(F32)
    other = lax.dynamic_index_in_dim(part, 1 - chip, 0, keepdims=False).astype(BF16)
    summed = lax.dynamic_index_in_dim(part, chip, 0, keepdims=False)
    summed = summed + lax.ppermute(other, "orb", [(i, i ^ 2) for i in range(4)]).astype(F32)
    return last, summed.astype(BF16)


def solution(mesh):
    in_specs = (
        P("dom", "orb"),
        P("dom", "orb"),
        P("dom", "orb"),
        P("dom"),
        P(),
        P("dom"),
        P("dom", None),
        P("dom", None),
        P("orb", "dom"),
        P(),
    )
    out_specs = (P("dom", "orb"), P(("dom", "orb"), None))
    return jax.shard_map(
        on_device, mesh=mesh, in_specs=in_specs, out_specs=out_specs, check_vma=False
    )
```

```python
import jax
import jax.numpy as jnp
import numpy as np
from jax import lax
from jax.experimental import pallas as pl
from jax.experimental.pallas import tpu as pltpu
from jax.sharding import PartitionSpec as P

PANELS = 4
STEPS = 4
RIDE = 1
RING = 4
LAYERS = 8
GROUPS = 2
SLOTS = 3
OWN = 1
CELLS = 4
NPC = 343
CPAD = 384
STACK = CELLS * CPAD
BND = 64
RIM = 2 * BND
LANES = 128
BND_ROW = STACK // LANES
POT_ROW = BND_ROW + 1
META = 24
HALF = 0.5
CENTER = 0.5
F32 = jnp.float32
BF16 = jnp.bfloat16


def dot(left, right):
    return jnp.dot(left, right, preferred_element_type=F32)


def dot_t(left, right):
    return lax.dot_general(left, right, (((1,), (1,)), ((), ())), preferred_element_type=F32)


def split(x):
    hi = x.astype(BF16)
    return hi, (x - hi.astype(F32)).astype(BF16)


def split_exact(x):
    hi = x.astype(BF16)
    return hi, x - hi.astype(F32)


def one_hot(index, shape, dim, first=0):
    places = lax.broadcasted_iota(jnp.int32, shape, dim) + first
    return jnp.where(index == places, 1.0, 0.0).astype(BF16)


def outset_kernel(sel, *refs):
    tables, vectors, (meta, both, edge), held, sems = refs[0:4], refs[4:6], refs[6:9], refs[9:13], refs[13:]
    copies = [pltpu.make_async_copy(table, here, sem) for table, here, sem in zip(tables, held, sems)]
    copies += [
        pltpu.make_async_copy(vector, both.at[0 : vector.shape[0], place * LANES : (place + 1) * LANES], sems[4 + place])
        for place, vector in enumerate(vectors)
    ]
    for copy in copies:
        copy.start()
    for copy in copies[:4]:
        copy.wait()
    connectivity, boundary, potential, cell_scale = held
    meta[...] = jnp.full(meta.shape, -1.0, F32)
    conn = connectivity[...].astype(F32)
    per_cell = CPAD // LANES
    for cell in range(CELLS):
        for part in range(per_cell):
            first, last = part * LANES, min((part + 1) * LANES, NPC)
            meta[cell * per_cell + part : cell * per_cell + part + 1, 0 : last - first] = conn[cell : cell + 1, first:last]
    lists = boundary[...].astype(F32)
    meta[BND_ROW : BND_ROW + 1, :] = jnp.concatenate([lists[0:1], lists[1:2]], axis=1)
    meta[POT_ROW : POT_ROW + potential.shape[0], :] = potential[...].astype(F32)
    meta[POT_ROW + potential.shape[0] : POT_ROW + potential.shape[0] + 1, 0:CELLS] = cell_scale[...]
    rows = vectors[0].shape[0]
    high, rest = split_exact(meta[...])
    middle, low = split_exact(rest)
    both[rows : rows + META, :] = jnp.concatenate([high, middle], axis=1)
    both[rows + META : rows + 2 * META, :] = jnp.concatenate([low.astype(BF16), jnp.zeros_like(high)], axis=1)
    chosen = one_hot(jnp.transpose(meta[...]).astype(jnp.int32)[:, BND_ROW : BND_ROW + 1], (RIM, rows), 1)
    for copy in copies[4:]:
        copy.wait()
    values = dot(chosen, both[0:rows, 0:LANES]).astype(BF16)
    edge[...] = jnp.where(sel[4, 0] == 1, values[:BND], values[BND:])


def prepare_kernel(rows, meta, stiff, *refs):
    if len(refs) == 10:
        direct, scatter, finish, pack, corner, potential, ready, taken, column, padded = refs
        padded[...] = jnp.zeros(padded.shape, F32)
        padded[0:NPC, 0:NPC] = stiff[...].astype(F32)
        ready[...] = padded[...].astype(BF16)
        stiff = ready
    else:
        arrived = meta
        direct, scatter, finish, pack, corner, potential, meta, taken, column = refs
        first = arrived[rows : rows + META, :].astype(F32)
        second = arrived[rows + META : rows + 2 * META, 0:LANES].astype(F32)
        meta[...] = first[:, 0:LANES] + first[:, LANES : 2 * LANES] + second
    k = stiff[...]
    rowed = meta[...].astype(jnp.int32)
    turned = jnp.transpose(meta[...])
    coled = turned.astype(jnp.int32)
    scales = meta[POT_ROW + rows // LANES :, :]
    per_cell = CPAD // LANES
    out_row = []
    spread_rim = []
    for cell in range(CELLS):
        factor = scales[0:1, cell : cell + 1]
        rim_in = []
        rim_out = []
        for part in range(cell * per_cell, (cell + 1) * per_cell):
            here = slice(part * LANES, (part + 1) * LANES)
            index = coled[:, part : part + 1]
            taken[here, :] = one_hot(index, (LANES, rows), 1)
            rim_in.append(one_hot(index, (LANES, RIM), 1, rows))
            index_t = rowed[part : part + 1, :]
            scatter[:, here] = one_hot(index_t, (rows, LANES), 0)
            rim_out.append(one_hot(index_t, (RIM, LANES), 0, rows))
        cells = slice(cell * CPAD, (cell + 1) * CPAD)
        column[cells, :] = jnp.concatenate(split(dot(k, jnp.concatenate(rim_in, axis=0)) * factor), axis=1)
        direct[cells, :] = dot(k, taken[cells, :]).astype(BF16)
        rim_out = jnp.concatenate(rim_out, axis=1)
        spread_rim.append(rim_out)
        out_row.append(jnp.concatenate(split(dot(rim_out, k) * factor), axis=0))
    ghost = dot(scatter[...], column[...])
    ghost_hi, ghost_lo = split(ghost[:, :RIM] + ghost[:, RIM:])
    place = one_hot(rowed[BND_ROW : BND_ROW + 1, :], (rows, RIM), 0)
    finish[:, 0:RIM] = ghost_hi
    finish[:, RIM : 2 * RIM] = ghost_lo
    finish[:, 2 * RIM : 3 * RIM] = place
    finish[:, 3 * RIM : 4 * RIM] = place
    rim = dot(jnp.concatenate(spread_rim, axis=1), column[...])
    corner_hi, corner_lo = split(rim[:, :RIM] + rim[:, RIM:])
    corner[0:RIM, :] = corner_hi
    corner[RIM : 2 * RIM, :] = corner_lo
    out = dot(jnp.concatenate(out_row, axis=1), taken[...])
    out_hi, out_lo = split(out[:RIM] + out[RIM:])
    pack[0:RIM, :] = out_hi
    pack[RIM : 2 * RIM, :] = out_lo
    pack[2 * RIM :, :] = one_hot(coled[:, BND_ROW : BND_ROW + 1], (RIM, rows), 1)
    for part in range(rows // LANES):
        values = turned[:, POT_ROW + part : POT_ROW + part + 1]
        potential[part * LANES : (part + 1) * LANES, :] = jnp.broadcast_to(values, (LANES, LANES)).astype(BF16)


def write_rims(slot, pack, field, rims, up, down):
    sums = dot(pack, field)
    terms = (sums[:RIM] + sums[RIM : 2 * RIM]).astype(BF16)
    values = sums[2 * RIM :].astype(BF16)
    rims[slot] = values
    down[slot, 0:BND, :] = values[:BND]
    down[slot, BND:RIM, :] = terms[:BND]
    up[slot, 0:BND, :] = values[BND:]
    up[slot, BND:RIM, :] = terms[BND:]


def first_kernel(rows, *refs):
    packs, fields, corners, (rims, up, down) = refs[0:3], refs[3:6], refs[6:9], refs[9:]
    for slot in range(SLOTS):
        write_rims(slot, packs[slot][...], fields[slot][0:rows, 0:LANES], rims, up, down)
        corner = corners[slot]
        down[slot, RIM : RIM + BND, :] = corner[0:BND, :]
        down[slot, RIM + BND : 2 * RIM, :] = corner[RIM : RIM + BND, :]
        up[slot, RIM : RIM + BND, :] = corner[BND:RIM, :]
        up[slot, RIM + BND : 2 * RIM, :] = corner[RIM + BND : 2 * RIM, :]


def local_values(meta, direct, scatter, current, previous, potential, pieces):
    rows, columns = current.shape
    scales = meta[POT_ROW + rows // LANES :, :]
    for cell in range(CELLS):
        cells = slice(cell * CPAD, (cell + 1) * CPAD)
        product = dot(direct[cells, :], current) * scales[0:1, cell : cell + 1]
        pieces[cells, :] = jnp.concatenate(split(product), axis=1)
    terms = dot(scatter[...], pieces[...])
    terms = terms[:, :columns] + terms[:, columns:]
    wide = current.astype(F32)
    applied = terms + potential[...].astype(F32) * wide
    return HALF * (applied - CENTER * wide) - previous.astype(F32)


def local_kernel(slots, step, views, sel, *refs):
    count = len(slots)
    groups = [refs[i * count : (i + 1) * count] for i in range(6)]
    base, pieces = refs[6 * count :]
    for place, slot in enumerate(slots):
        meta, direct, scatter, field, previous, potential = (group[place] for group in groups)

        def body(place=place, meta=meta, direct=direct, scatter=scatter, field=field, previous=previous, potential=potential):
            now, before = views[place]
            base[place] = local_values(meta, direct, scatter, now(field), before(previous), potential, pieces)

        guard(sel, step, slot, body)


def guard(sel, step, slot, body):
    if slot == OWN or step == 0:
        body()
    else:
        pl.when(sel[5, slot] <= STEPS - step)(body)


def new_field(slot, sel, base, finish, rims, low, high, across, mats_low, mats_high, edge):
    from_low, from_high = low.at[sel[0, slot]], high.at[sel[1, slot]]
    mat_low, mat_high = mats_low.at[sel[0, slot]], mats_high.at[sel[1, slot]]
    below, above = from_low[0:BND, :], from_high[0:BND, :]
    if edge is not None and slot == 0:
        below = jnp.where(sel[4, 0] == 1, edge[...], below)
    if edge is not None and slot == SLOTS - 1:
        above = jnp.where(sel[4, 1] == 1, edge[...], above)
    ghosts = jnp.concatenate([below, above], axis=0)
    own = rims[slot]
    to_low = jnp.concatenate([across[sel[2, slot], BND:RIM, :], own[:BND]], axis=0)
    to_high = jnp.concatenate([own[BND:], across[sel[3, slot], 0:BND, :]], axis=0)
    back_low = from_low[BND:RIM, :].astype(F32) + sum_rims(dot(mat_low[RIM : 2 * RIM, :], to_low))
    back_high = from_high[BND:RIM, :].astype(F32) + sum_rims(dot(mat_high[RIM : 2 * RIM, :], to_high))
    back_hi, back_lo = split(jnp.concatenate([back_low, back_high], axis=0))
    right = jnp.concatenate([ghosts, ghosts, back_hi, back_lo], axis=0)
    return (base + HALF * dot(finish[...], right)).astype(BF16)


def sum_rims(x):
    return x[:BND] + x[BND:]


def step_kernel(step, sel, base_own, base_sides, *refs):
    if step == RIDE:
        refs, held = refs[:-5] + refs[-4:], refs[-5]
        for ref in refs[-3:]:
            for row in range(2):
                for col in range(2):
                    tile = held[row * RIM : (row + 1) * RIM, col * RIM : (col + 1) * RIM]
                    ref[SLOTS + 2 * row + col] = tile
    finishes, packs, refs = refs[0:3], refs[3:6], refs[6:]
    rims, low, high, across, mats_low, mats_high = refs[:6]
    refs = refs[6:]
    edge = None
    if step == 0:
        edge, refs = refs[0], refs[1:]
    field, new_rims, up, down = refs
    for slot in (0, 2, 1):

        def body(slot=slot):
            base = base_own[0] if slot == OWN else base_sides[slot // 2]
            following = new_field(slot, sel, base, finishes[slot], rims, low, high, across, mats_low, mats_high, edge)
            field[slot] = following
            write_rims(slot, packs[slot][...], following, new_rims, up, down)

        guard(sel, step, slot, body)
        if slot != OWN and step > 0:

            @pl.when(sel[5, slot] > STEPS - step)
            def _(slot=slot):
                for ref in (new_rims, up, down):
                    ref[slot] = jnp.zeros(ref.shape[1:], ref.dtype)


def others_kernel(sel, held, low, across, high, others, product, weights, panels):
    width = held.shape[1]
    for step, part in enumerate((held, low, across, high)):
        first = jnp.bitwise_and(sel[4, 2] - step, RING - 1) * width
        for row in range(2):
            for col in range(2):
                there = pl.ds(pl.multiple_of(first + col * RIM, RIM), RIM)
                rows = slice(row * RIM, (row + 1) * RIM)
                panels[rows, there] = part[rows, col * RIM : (col + 1) * RIM] if step == 0 else part[SLOTS + 2 * row + col]
    weights[...] = panels[:, 0:LANES]
    product[...] = dot_t(others[...], panels[:, LANES:])


def last_kernel(sel, base, finish, rims, low, high, across, mats_low, mats_high, weights, others_part, field, kept, part):
    following = new_field(OWN, sel, base[0], finish, rims, low, high, across, mats_low, mats_high, None)
    field[...] = following
    share = kept.shape[1]
    for chip in range(2):
        for core, to in ((sel[6, 0], kept), (1 - sel[6, 0], part)):
            here = pl.ds(pl.multiple_of((2 * chip + core) * share, share), share)
            to[chip] = (dot_t(field[here, :], weights[...]) + others_part[here, :]).astype(to.dtype)


def shape(*dims, kind=BF16):
    return jax.ShapeDtypeStruct(dims, kind)


VMEM = pl.BlockSpec(memory_space=pltpu.VMEM)
SMEM = pl.BlockSpec(memory_space=pltpu.SMEM)


def call(kernel, name, micros, operands, out_shape, scratch=(), mib=6):
    specs = [SMEM if op.shape == (7, SLOTS) else VMEM for op in operands]
    cost = pl.CostEstimate(flops=int(micros * 1.1e9), bytes_accessed=1 << 16, transcendentals=0)
    return pl.pallas_call(
        kernel,
        in_specs=specs,
        out_specs=jax.tree.map(lambda _: VMEM, out_shape),
        out_shape=out_shape,
        scratch_shapes=scratch,
        compiler_params=pltpu.CompilerParams(vmem_limit_bytes=mib << 20),
        cost_estimate=cost,
        name=name,
    )(*operands)


def prepare(meta, stiff, rows, own=False):
    extra = [shape(CPAD, CPAD)] if own else [shape(META, LANES, kind=F32)]
    return call(
        lambda *refs: prepare_kernel(rows, *refs),
        "prepare",
        0.1,
        [meta, stiff],
        [
            shape(STACK, rows),
            shape(rows, STACK),
            shape(rows, 4 * RIM),
            shape(3 * RIM, rows),
            shape(2 * RIM, RIM),
            shape(rows, LANES),
        ]
        + extra,
        [pltpu.VMEM((STACK, rows), BF16), pltpu.VMEM((STACK, 2 * RIM), BF16)]
        + ([pltpu.VMEM((CPAD, CPAD), F32)] if own else []),
        mib=10,
    )


def local_part(slots, step, sel, metas, made, fields, previous):
    rows = made[OWN][1].shape[0]
    views = [(fields[s][1], previous[s][1]) for s in slots]
    operands = [sel]
    operands += [metas[s] for s in slots]
    operands += [made[s][0] for s in slots]
    operands += [made[s][1] for s in slots]
    operands += [fields[s][0] for s in slots]
    operands += [previous[s][0] for s in slots]
    operands += [made[s][5] for s in slots]
    return call(
        lambda *refs: local_kernel(slots, step, views, *refs),
        "local_part",
        0.3 * len(slots),
        operands,
        shape(len(slots), rows, LANES, kind=F32),
        [pltpu.VMEM((STACK, 2 * LANES), BF16)],
    )


def place_of(device):
    return device // (RING * GROUPS), device // RING % GROUPS, device % RING


def device_at(layer, group, spot):
    return (layer % LAYERS * GROUPS + group % GROUPS) * RING + spot % RING


def shift(x, layers, groups, spots):
    pairs = []
    for device in range(LAYERS * GROUPS * RING):
        layer, group, spot = place_of(device)
        pairs.append((device, device_at(layer + layers, group + groups, spot + spots)))
    return lax.ppermute(x, "dom", pairs)


def swap(x, layers, spots):
    pairs = []
    for device in range(LAYERS * GROUPS * RING):
        layer, group, spot = place_of(device)
        pairs.append((device, device_at(layer ^ layers, group, spot ^ spots)))
    return lax.ppermute(x, "dom", pairs)


def along(x, steps):
    count = lax.axis_size("dom")
    return lax.ppermute(x, "dom", [(i, i + steps) for i in range(count) if 0 <= i + steps < count])


def turn(x, steps):
    count = lax.axis_size("orb")
    return lax.ppermute(x, "orb", [(i, (i + steps) % count) for i in range(count)])


def together(*values):
    return lax.optimization_barrier(values)


def panels_in_ring(rotation, panel_ids):
    layer, group, spot = place_of(lax.axis_index("dom"))
    mine = rotation.T
    width = mine.shape[1] // RING
    wanted = []
    for step in range(RING):
        part = lax.dynamic_slice_in_dim(mine, (spot ^ step) * width, width, 1)
        part = swap(part, 0, step) if step else part
        holder = device_at(layer, group, spot ^ step)
        wanted.append(jnp.where((panel_ids == holder)[:, None, None], part[None], jnp.zeros_like(part)[None]))
    return sum(wanted[1:], wanted[0]).reshape(PANELS * mine.shape[0], width)


def choices():
    table = np.zeros((RING, 2, 7, SLOTS), np.int32)
    for spot in range(RING):
        for slot in range(SLOTS):
            below, above = max(slot - 1, 0), min(slot + 1, SLOTS - 1)
            table[spot, :, 0, slot] = below if spot == 0 else slot
            table[spot, :, 1, slot] = above if spot == RING - 1 else slot
            table[spot, :, 2, slot] = below if spot < 2 else slot
            table[spot, :, 3, slot] = above if spot >= 2 else slot
            table[spot, :, 5, slot] = (RING - spot, 0, spot + 1)[slot]
        table[spot, :, 4, 0] = spot == 0
        table[spot, :, 4, 1] = spot == RING - 1
        table[spot, :, 4, 2] = spot
        table[spot, 1, 6, 0] = 1
    return table


def on_device(
    y_prev,
    y_cur,
    others,
    potential,
    stiffness,
    cell_scale,
    connectivity,
    boundary,
    rotation,
    panel_ids,
):
    rows, columns = y_cur.shape
    spot = lax.axis_index("dom") % RING
    sel = jnp.asarray(choices())[spot, lax.axis_index("orb") % 2]

    tables = [connectivity, boundary, potential.reshape(-1, LANES), cell_scale.reshape(1, -1)]
    sent_rows = rows + 2 * META
    own_meta, both, edge = pl.pallas_call(
        outset_kernel,
        grid=(1,),
        in_specs=[SMEM] + [pl.BlockSpec(memory_space=pl.ANY)] * 6,
        out_specs=[pl.BlockSpec(dims, lambda i: (0, 0)) for dims in ((META, LANES), (sent_rows, 2 * LANES), (BND, LANES))],
        out_shape=[shape(META, LANES, kind=F32), shape(sent_rows, 2 * columns), shape(BND, columns)],
        scratch_shapes=[pltpu.VMEM(t.shape, t.dtype) for t in tables] + [pltpu.SemaphoreType.DMA] * 6,
        compiler_params=pltpu.CompilerParams(vmem_limit_bytes=60 << 20),
        cost_estimate=pl.CostEstimate(flops=10**8, bytes_accessed=1 << 16, transcendentals=0),
        name="outset",
    )(sel, *tables, y_cur, y_prev)
    sides = [along(both, RING), both, along(both, -RING)]
    held = panels_in_ring(rotation, panel_ids)

    current = [(side, lambda ref: ref[0:rows, 0:LANES]) for side in sides]
    previous = [(side, lambda ref: ref[0:rows, LANES : 2 * LANES]) for side in sides]

    received = swap(held, 1, 0)
    *parts, stiff = prepare(own_meta, stiffness, rows, own=True)
    made = [None, list(parts), None]
    count = lax.axis_size("dom")
    pairs = [(i, i + RING + 1) for i in range(count) if i % RING == RING - 1 and i + RING + 1 < count]
    pairs += [(i, i - RING - 1) for i in range(count) if i % RING == 0 and i - RING - 1 >= 0]
    edge = lax.ppermute(edge, "dom", pairs)
    made[0] = list(prepare(sides[0], stiff, rows))
    made[0][3], held = together(made[0][3], held)
    held = held + received
    received = swap(held, 2, 0)
    made[2] = list(prepare(sides[2], stiff, rows))
    metas = [made[0][6], own_meta, made[2][6]]
    made[OWN][3], made[2][3], held = together(made[OWN][3], made[2][3], held)
    held = held + received

    finishes = [m[2] for m in made]
    packs = [m[3] for m in made]
    rims, up, down = call(
        lambda *refs: first_kernel(rows, *refs),
        "first_rims",
        1,
        packs + sides + [m[4] for m in made],
        [shape(SLOTS, RIM, columns), shape(SLOTS, 2 * RIM, columns), shape(SLOTS, 2 * RIM, columns)],
    )
    held, up, down, rims, own_both = together(held, up, down, rims, both)
    current[OWN] = (own_both, current[OWN][1])
    previous[OWN] = (own_both, previous[OWN][1])

    for step in range(STEPS):
        low = shift(up, 0, 0, 1)
        high = shift(down, 0, 0, -1)
        across = shift(rims, 0, 0, 2)
        if step == 0:
            mats = [low, high]
            held = held + swap(held, 4, 0)
        elif step == 1:
            held = held + shift(held, 0, 1, 0)
        elif step == RIDE + 1:
            rides = [low, across, high]
        if step == STEPS - 1:
            others_part, weights = call(
                others_kernel,
                "others_part",
                0.2,
                [sel, held, *rides, others],
                [shape(rows, held.shape[0], kind=F32), shape(held.shape[0], columns)],
                [pltpu.VMEM((held.shape[0], RING * held.shape[1]), BF16)],
                mib=8,
            )
            base = local_part([OWN], step, sel, metas, made, current, previous)
            break
        base_sides = local_part([0, 2], step, sel, metas, made, current, previous)
        base_own = local_part([OWN], step, sel, metas, made, current, previous)
        base_sides, base_own, held = together(base_sides, base_own, held)
        operands = [sel, base_own, base_sides] + finishes + packs + [rims, low, high, across] + mats
        field, rims, up, down = call(
            lambda *refs, step=step: step_kernel(step, *refs),
            "step",
            2,
            operands + ([edge] if step == 0 else []) + ([held] if step == RIDE else []),
            [shape(SLOTS, rows, columns)] + [shape(SLOTS + (4 if step == RIDE else 0), RIM, columns)] * 3,
        )
        held, up, down, rims = together(held, up, down, rims)
        previous = current
        current = [(field, lambda ref, s=s: ref[s]) for s in range(SLOTS)]

    share = rows // lax.axis_size("orb")
    last, kept, part = call(
        last_kernel,
        "last_step",
        2,
        [sel, base, finishes[OWN], rims, low, high, across] + mats + [weights, others_part],
        [
            shape(rows, columns),
            shape(2, share, others_part.shape[1], kind=F32),
            shape(2, share, others_part.shape[1]),
        ],
    )
    me = lax.axis_index("orb")
    chip = me // 2
    part = kept + lax.ppermute(part, "orb", [(i, i ^ 1) for i in range(4)]).astype(F32)
    other = lax.dynamic_index_in_dim(part, 1 - chip, 0, keepdims=False).astype(BF16)
    summed = lax.dynamic_index_in_dim(part, chip, 0, keepdims=False)
    summed = summed + lax.ppermute(other, "orb", [(i, i ^ 2) for i in range(4)]).astype(F32)
    return last, summed.astype(BF16)


def solution(mesh):
    in_specs = (
        P("dom", "orb"),
        P("dom", "orb"),
        P("dom", "orb"),
        P("dom"),
        P(),
        P("dom"),
        P("dom", None),
        P("dom", None),
        P("orb", "dom"),
        P(),
    )
    out_specs = (P("dom", "orb"), P(("dom", "orb"), None))
    return jax.shard_map(
        on_device, mesh=mesh, in_specs=in_specs, out_specs=out_specs, check_vma=False
    )
```
